256 devices in a mesh: quad: 8 (over x, core), leaf: 32 (over y, z).
Axes of the slice: x: 4, y: 4, z: 8, core: 2. Of those that a mesh axis runs over, the one named last changes fastest.
Arguments:
- rhs_leaf: bfloat16 [32768, 128], P('leaf'), may hold values from -6 to 6
- rhs_mid: bfloat16 [1024, 128], P('leaf'), may hold values from -6 to 6
- rhs_root: bfloat16 [1024, 128], P('leaf'), may hold values from -6 to 6
- leaf_inv: bfloat16 [16, 2, 32768, 1024], P('quad', None, 'leaf'), may hold values from -0.125 to 0.125
- leaf_couple: bfloat16 [16, 2, 4096, 1024], P('quad', None, 'leaf'), may hold values from -0.125 to 0.125
- row_lists: int32 [32, 128], P('leaf'), may hold values from 0 to 511, as said below
- leaf_sizes: int32 [32], P('leaf'), may hold values from 1 to 1024, 20480 in all
- mid_inv: bfloat16 [16, 2, 1024, 512], P('quad', None, 'leaf'), may hold values from -0.1875 to 0.1875
- mid_root: bfloat16 [16, 2, 1024, 1024], P('quad', None, 'leaf'), may hold values from -0.25 to 0.25
- root_inv: bfloat16 [16, 2, 1024, 1024], P('quad', None, 'leaf'), may hold values from -0.125 to 0.125
Outputs:
- moments_leaf: float32 [8, 32768, 128], P('quad', 'leaf')
- moments_mid: float32 [8, 1024, 128], P('quad', 'leaf')
- moments_root: float32 [8, 1024, 128], P('quad', 'leaf')
The draws below stay inside these ranges and needn't reach their ends.
Inputs may be any that keep to these rules, and one draw needn't show every extreme that they name: `row_lists`: each row holds 128 distinct rows of the parent supernode's 512. Leaf supernode l is live on its leading leaf_sizes[l] rows; the sizes sum to 20480.
All inputs are finite; a program needn't handle non-finite values. No bound on the sum of `leaf_sizes` on one device may be relied on, other than what follows from the above.
Results may differ from the reference program's by a relative error of at most 0.019.
Values may be sent and summed in bfloat16 or wider, within the bound.
A program may use at most 64 MiB of HBM per device.

```python
import math
import jax
import jax.numpy as jnp
import numpy as np
from jax import lax

PROBES = 128
MOMENTS = 8
LEAF_ROWS = 1024
QPOINTS = 16
GROUP = 16
MID_SEP = 512
MID_ROWS = 1024
COUPLE = 128
COUPLE_ALL = 4096
ROOT_SEP = 1024
LEAF_ALL = 32768
N_LEAF = 32


def draw_row_lists(key, part):
    key = jax.random.fold_in(key, 11)
    leaf_keys = jax.random.split(key, N_LEAF)
    scores = jax.vmap(lambda single: jax.random.permutation(single, MID_SEP))(leaf_keys).astype(jnp.int32)
    leaf_ids = jnp.arange(N_LEAF, dtype=jnp.int32)[:, None]
    row_ids = jnp.arange(MID_SEP, dtype=jnp.int32)[None, :]
    scores = jnp.where((leaf_ids == 0) & (row_ids == 0), -2, scores)
    scores = jnp.where((leaf_ids == 0) & (row_ids == MID_SEP - 1), -1, scores)
    ordering = jnp.argsort(scores, axis=1, stable=True)
    return ordering[:, :COUPLE].astype(jnp.int32)


def spiked(drawn, rng, source, target, parts, factor):
    owner, partner = [(jnp.arange(drawn.shape[position]) // (drawn.shape[position] // parts)).reshape([-1 if axis == position else 1 for axis in range(drawn.ndim)]) for position in (source, target)]
    chosen = jax.random.permutation(rng, parts)[partner]
    strong = (owner == chosen) | (owner == (partner + parts // 2) % parts)
    return jnp.where(strong, factor * drawn, drawn)


def block_scale(stream_key, extent, cuts, smallest, largest):
    def one(position, shards_of):
        draws = jax.random.uniform(jax.random.fold_in(jax.random.fold_in(stream_key, 6), position), (shards_of,), jnp.float32, smallest / len(cuts), largest / len(cuts))
        return jnp.repeat(jnp.exp(draws), extent[position] // shards_of).reshape((-1,) + (1,) * (len(extent) - position - 1))

    loudness = one(*cuts[0])
    for cut in cuts[1:]:
        loudness = loudness * one(*cut)
    return loudness


def profile(number_of, total, bound, slope):
    weights = [(1 << 20) // math.isqrt(rank ** slope) + 1 for rank in range(2, number_of + 1)]
    surplus, given = total - bound - (number_of - 1), [1] * (number_of - 1)
    while surplus > 0:
        movable = [i for i in range(number_of - 1) if given[i] < bound]
        mass, budget = sum([weights[i] for i in movable]), surplus
        for i in movable:
            more = min(bound - given[i], max(1, budget * weights[i] // mass), surplus)
            given[i] = given[i] + more
            surplus = surplus - more
    return np.array([bound] + given)


def ragged(key, count, total, bound, lean):
    if count == 2:
        one = jax.random.randint(key, (), max(1, total - bound), min(bound, total - 1) + 1)
        return jnp.stack([one, total - one])
    lengths = jnp.asarray(profile(count, total, bound, lean), jnp.int32)
    twos = (count - 1) // 2
    donor, sink = lengths[1:1 + 2 * twos:2], lengths[2:2 + 2 * twos:2]
    room = jnp.minimum(donor - 1, bound - sink)
    moved = jax.random.randint(jax.random.fold_in(key, 1), (twos,), 0, 1 << 20) % (room + 1)
    lengths = lengths.at[1:1 + 2 * twos:2].set(donor - moved).at[2:2 + 2 * twos:2].set(sink + moved)
    return lengths[jax.random.permutation(jax.random.fold_in(key, 2), count)]


def noise(stream_key, dims, width, reach, cuts=(), held_as=jnp.bfloat16):
    drawn = jax.random.normal(stream_key, dims, jnp.float32) * width
    if len(cuts) > 0:
        drawn = block_scale(stream_key, dims, cuts, -0.22, 0.18) * drawn
    return jnp.clip(drawn, min=-reach, max=reach).astype(held_as)


def bell_draw_with(own_key, shape, scale, limit, pieces, heavy, held_as=jnp.bfloat16):
    result = scale * jax.random.normal(own_key, shape, jnp.float32)
    if pieces:
        result = result * block_scale(own_key, shape, pieces, -0.22, 0.18)
    return jnp.clip(spiked(result, jax.random.fold_in(own_key, 3), *heavy), -limit, limit).astype(held_as)


def setup_inputs(seed: int = 0) -> dict:
    key_of = jax.random.split(jax.random.key(seed), 11)
    rhs_leaf = noise(key_of[0], (LEAF_ALL, PROBES), 1.0, 6.0, ((0, 32),))
    rhs_mid = noise(key_of[1], (MID_ROWS, PROBES), 1.0, 6.0, ((0, 32),))
    rhs_root = noise(key_of[2], (ROOT_SEP, PROBES), 1.0, 6.0, ((0, 32),))
    leaf_inv = noise(key_of[3], (QPOINTS, 2, LEAF_ALL, LEAF_ROWS), (2 * LEAF_ROWS) ** -0.5, 0.125, ((0, 8), (2, 32)))
    leaf_couple = noise(key_of[4], (QPOINTS, 2, COUPLE_ALL, LEAF_ROWS), (2 * LEAF_ROWS) ** -0.5, 0.125, ((0, 8), (2, 32)))
    row_lists = draw_row_lists(jax.random.fold_in(key_of[10], 71), 0)
    leaf_sizes = ragged(key_of[6], N_LEAF, LEAF_ROWS * N_LEAF * 5 // 8, LEAF_ROWS, 2).astype(jnp.int32)
    mid_inv = noise(key_of[7], (QPOINTS, 2, MID_ROWS, MID_SEP), (2 * MID_SEP) ** -0.5, 0.1875, ((0, 8), (2, 32)))
    mid_root = bell_draw_with(key_of[8], (QPOINTS, 2, MID_ROWS, ROOT_SEP), (2 * MID_ROWS) ** -0.5, 0.25, ((0, 8), (2, 32)), (2, 3, 32, 2.75))
    root_inv = noise(key_of[9], (QPOINTS, 2, ROOT_SEP, ROOT_SEP), (2 * ROOT_SEP) ** -0.5, 0.125, ((0, 8), (2, 32)))
    return dict(rhs_leaf=rhs_leaf, rhs_mid=rhs_mid, rhs_root=rhs_root, leaf_inv=leaf_inv, leaf_couple=leaf_couple, row_lists=row_lists, leaf_sizes=leaf_sizes, mid_inv=mid_inv, mid_root=mid_root, root_inv=root_inv)


def rounded(values):
    return lax.optimization_barrier(values.astype(jnp.bfloat16)).astype(jnp.float32)


def complex_product(form, matrix, vector):
    def single(left, right):
        return jnp.einsum(form, left, right)
    real_part = single(matrix[0], vector[0]) - single(matrix[1], vector[1])
    imag_part = single(matrix[0], vector[1]) + single(matrix[1], vector[0])
    return jnp.stack([real_part, imag_part])


def embedded(values):
    real_part = values.astype(jnp.float32)
    return jnp.stack([real_part, jnp.zeros_like(real_part)])


def reference(rhs_leaf, rhs_mid, rhs_root, leaf_inv, leaf_couple, row_lists, leaf_sizes, mid_inv, mid_root, root_inv):
    live_mask = (jnp.arange(LEAF_ROWS, dtype=jnp.int32)[None, :] < leaf_sizes[:, None]).astype(jnp.float32)
    live_rows = live_mask[None, :, :, None]
    source = rhs_leaf.astype(jnp.float32).reshape(N_LEAF, LEAF_ROWS, PROBES) * live_mask[:, :, None]
    parent = jnp.arange(N_LEAF, dtype=jnp.int32) // GROUP
    targets = (parent[:, None] * MID_SEP + row_lists).reshape(-1).astype(jnp.int32)
    mid_source = embedded(rhs_mid)
    root_source = embedded(rhs_root)
    orders = jnp.arange(MOMENTS, dtype=jnp.float32) + 1.0

    def one_point(carry, inputs):
        inv_leaf, couple, inv_mid, to_root, inv_root, point = inputs
        inv_leaf = inv_leaf.astype(jnp.float32).reshape(2, N_LEAF, LEAF_ROWS, LEAF_ROWS)
        couple = couple.astype(jnp.float32).reshape(2, N_LEAF, COUPLE, LEAF_ROWS)
        inv_mid = inv_mid.astype(jnp.float32).reshape(2, 2, MID_SEP, MID_SEP)
        to_root = to_root.astype(jnp.float32)
        inv_root = inv_root.astype(jnp.float32)
        forward_leaf = rounded(jnp.einsum('alnm,lmp->alnp', inv_leaf, source) * live_rows)
        terms = complex_product('lrn,lnp->lrp', couple, forward_leaf).reshape(2, COUPLE_ALL, PROBES)
        sep_terms = jnp.zeros((2, MID_ROWS, PROBES), jnp.float32).at[:, targets].add(terms)
        residual_mid = rounded(mid_source - sep_terms)
        forward_mid = complex_product('jmn,jnp->jmp', inv_mid, residual_mid.reshape(2, 2, MID_SEP, PROBES))
        forward_mid = rounded(forward_mid.reshape(2, MID_ROWS, PROBES))
        residual_root = rounded(root_source - complex_product('mr,mp->rp', to_root, forward_mid))
        forward_root = rounded(complex_product('rs,sp->rp', inv_root, residual_root))
        backward_root = rounded(complex_product('sr,sp->rp', inv_root, forward_root))
        update_mid = rounded(forward_mid - complex_product('mr,rp->mp', to_root, backward_root))
        backward_mid = complex_product('jmn,jmp->jnp', inv_mid, update_mid.reshape(2, 2, MID_SEP, PROBES))
        backward_mid = rounded(backward_mid.reshape(2, MID_ROWS, PROBES))
        picked = backward_mid[:, targets].reshape(2, N_LEAF, COUPLE, PROBES)
        update_leaf = rounded((forward_leaf - complex_product('lrn,lrp->lnp', couple, picked)) * live_rows)
        backward_leaf = complex_product('lmn,lmp->lnp', inv_leaf, update_leaf) * live_rows
        base = (point.astype(jnp.float32) + 0.5) * (2.0 * jnp.pi / QPOINTS)
        angles = base * orders
        weight_real = (4.0 / QPOINTS) * jnp.cos(angles)
        weight_imag = (4.0 / QPOINTS) * jnp.sin(angles)

        def weigh(values):
            return weight_real[:, None, None] * values[0][None] - weight_imag[:, None, None] * values[1][None]

        leaf_sum = carry[0] + weigh(backward_leaf.reshape(2, LEAF_ALL, PROBES))
        mid_sum = carry[1] + weigh(backward_mid)
        root_sum = carry[2] + weigh(backward_root)
        return (leaf_sum, mid_sum, root_sum), None

    initial = (jnp.zeros((MOMENTS, LEAF_ALL, PROBES), jnp.float32),
               jnp.zeros((MOMENTS, MID_ROWS, PROBES), jnp.float32),
               jnp.zeros((MOMENTS, ROOT_SEP, PROBES), jnp.float32))
    points = jnp.arange(QPOINTS, dtype=jnp.int32)
    final, unused = lax.scan(one_point, initial, (leaf_inv, leaf_couple, mid_inv, mid_root, root_inv, points))
    return (final[0], final[1], final[2])
```

```python
import functools
import math

import jax
import jax.numpy as jnp
import numpy as np
from jax import lax
from jax.experimental import pallas as pl
from jax.experimental.pallas import tpu as pltpu
from jax.sharding import PartitionSpec as P

MESH = pl.DeviceIdType.MESH
BF16 = jnp.bfloat16
F32 = jnp.float32

MOMENTS = 8
QPOINTS = 16
PROBES = 128
LEAF = 1024
COUPLE = 128
SEP = 512
ROOT = 1024
NX, NY, NZ, NC = 4, 4, 8, 2
OWN = 32
BLOCK = OWN * NZ
SLICE = 32
CHUNK = 256
CHUNKS = LEAF // CHUNK


def nt(left, right):
    return lax.dot_general(left, right, (((1,), (1,)), ((), ())), preferred_element_type=F32)


def nn(left, right):
    return lax.dot_general(left, right, (((1,), (0,)), ((), ())), preferred_element_type=F32)


def join(with_real, with_imag):
    half = with_real.shape[0] // 2
    return jnp.concatenate(
        [with_real[:half] - with_imag[half:], with_real[half:] + with_imag[:half]], axis=0
    )


def kernel(
    rhs_leaf,
    rhs_mid,
    rhs_root,
    leaf_inv,
    leaf_couple,
    row_list,
    leaf_size,
    mid_inv,
    mid_root,
    root_inv,
    weights,
    out_leaf,
    out_mid,
    out_root,
    inv_v,
    couple_v,
    source,
    forward,
    update,
    mid_f,
    couple_f,
    root_f,
    places,
    lists,
    rhs_mid_y,
    rhs_root_y,
    terms,
    terms_in,
    mid_part,
    mid_send,
    mid_recv,
    root_part,
    root_send,
    root_recv,
    back_send,
    back_recv,
    x_root,
    xmid_send,
    xmid_recv,
    x_mid,
    picked_send,
    picked,
    parts,
    own_sum,
    core_send,
    core_recv,
    chip_own,
    chip_send,
    chip_recv,
    small_send,
    small_recv,
    spread,
    rows_send,
    rows_recv,
    inv_sem,
    couple_sem,
    lists_sem,
    block_sem,
    pass_sem,
    terms_sem,
    mid_sem,
    root_sem,
    back_sem,
    xmid_sem,
    picked_sem,
    core_sem,
    chip_sem,
    small_sem,
    rows_sem,
    send_sem,
):
    quad, leaf = lax.axis_index("quad"), lax.axis_index("leaf")
    x, c = lax.div(quad, 2), lax.rem(quad, 2)
    y, z = lax.div(leaf, NZ), lax.rem(leaf, NZ)
    home = lax.div(z, 4)
    point = lax.rem(lax.div(z, 2), 2)
    group = 2 * lax.rem(z, 2) + c
    half = lax.rem(y, 2)
    size = leaf_size[0]
    sends = []
    counter = [0]

    def device(xx, cc, yy, zz):
        return (2 * xx + cc, NZ * yy + zz)

    def send(src, dst, recv, target):
        copy = pltpu.make_async_remote_copy(
            src_ref=src,
            dst_ref=dst,
            send_sem=send_sem.at[counter[0]],
            recv_sem=recv,
            device_id=target,
            device_id_type=MESH,
        )
        counter[0] += 1
        return copy

    def post(src, dst, recv, target):
        copy = send(src, dst, recv, target)
        copy.start()
        sends.append((None, copy))
        return copy

    def post_or_keep(src, dst, recv, cc, zz):
        mine = jnp.logical_and(cc == c, zz == z)
        copy = send(src, dst, recv, device(x, cc, y, zz))

        @pl.when(mine)
        def _():
            pltpu.make_async_copy(src, dst, recv).start()

        @pl.when(jnp.logical_not(mine))
        def _():
            copy.start()

        sends.append((mine, copy))

    def arrived(buffer, sem):
        pltpu.make_async_copy(buffer, buffer, sem).wait()

    for i in range(16):
        q, a, n = i // 8, i // 4 % 2, i % 4
        block = (q, a, pl.ds(n * 256, 256))
        pltpu.make_async_copy(leaf_inv.at[block], inv_v.at[block], inv_sem.at[i]).start()
    couple_load = pltpu.make_async_copy(leaf_couple, couple_v, couple_sem)
    couple_load.start()

    barrier = pltpu.get_barrier_semaphore()
    mates = []
    for i in range(1, NC * NZ):
        place = lax.rem(c * NZ + z + i, NC * NZ)
        mates.append(device(x, lax.div(place, NZ), y, lax.rem(place, NZ)))
    y_mates = [device(x, c, lax.rem(y + d, NY), z) for d in range(1, NY)]
    x_mates = [device(lax.rem(x + d, NX), c, y, z) for d in range(1, NX)]
    for mate in mates + y_mates + x_mates:
        pl.semaphore_signal(barrier, inc=1, device_id=mate, device_id_type=MESH)

    row_live = lax.broadcasted_iota(jnp.int32, (LEAF, PROBES), 0) < size
    masked = jnp.where(row_live, rhs_leaf[...].astype(F32), 0.0)
    source[...] = masked.T.astype(BF16)

    def forward_step(i, carry):
        q, a, n = lax.div(i, 8), lax.rem(lax.div(i, 4), 2), lax.rem(i, 4)
        rows = pl.ds(pl.multiple_of(n * 256, 256), 256)
        arrived(inv_v.at[q, a, rows], inv_sem.at[i])
        product = nt(source[...], inv_v[q, a, rows, :])
        live = lax.broadcasted_iota(jnp.int32, product.shape, 1) + n * 256 < size
        forward[q, pl.ds(pl.multiple_of(a * PROBES, PROBES), PROBES), rows] = jnp.where(
            live, product, 0.0
        ).astype(BF16)
        return carry

    def couple_step(q):
        terms_q = join(nt(forward[q], couple_v[q, 0]), nt(forward[q], couple_v[q, 1]))
        terms[q] = terms_q.astype(BF16).reshape(2, PROBES, COUPLE)
        for t in (2 * q, 2 * q + 1):
            for cc in range(NC):
                pg = 2 * (t % 2) + cc
                post_or_keep(
                    terms.at[q, :, pl.ds(pg * SLICE, SLICE), :],
                    terms_in.at[:, :, pl.ds(pl.multiple_of(z * COUPLE, COUPLE), COUPLE)],
                    terms_sem,
                    cc,
                    4 * c + t,
                )

    def spread_blocks(matrix, whole, sem):
        for t in range(4):
            for cc in range(NC):
                post_or_keep(
                    matrix.at[t // 2, cc],
                    whole.at[cc, pl.ds(pl.multiple_of(z * OWN, OWN), OWN), :],
                    sem,
                    cc,
                    4 * c + t,
                )

    def pass_on(whole, sem, pass_on_sem):
        arrived(whole.at[c], sem)
        return post(whole.at[c], whole.at[c], pass_on_sem, device(x, 1 - c, y, z))

    lax.fori_loop(0, 8, forward_step, 0)
    pl.semaphore_wait(barrier, len(mates) + len(y_mates) + len(x_mates))

    for d in range(NZ):
        for k, (src, dst) in enumerate(
            ((row_list, lists), (rhs_mid, rhs_mid_y), (rhs_root, rhs_root_y))
        ):
            if d == 0:
                pltpu.make_async_copy(src, dst.at[z], lists_sem.at[k]).start()
            else:
                post(src, dst.at[z], lists_sem.at[k], device(x, c, y, lax.rem(z + d, NZ)))
    spread_blocks(mid_inv, mid_f, block_sem.at[0])

    couple_load.wait()
    couple_step(0)
    lax.fori_loop(8, 16, forward_step, 0)
    couple_step(1)
    spread_blocks(mid_root, couple_f, block_sem.at[1])
    spread_blocks(root_inv, root_f, block_sem.at[2])

    arrived(lists, lists_sem.at[0])
    for l in range(NZ):
        sep_row = lax.broadcasted_iota(jnp.int32, (SEP, COUPLE), 0)
        places[:, l * COUPLE : (l + 1) * COUPLE] = (
            jnp.where(sep_row == lists[l], 1.0, 0.0).astype(BF16)
        )
    chosen = jnp.where(
        lax.broadcasted_iota(jnp.int32, (SLICE, PROBES), 1)
        == lax.broadcasted_iota(jnp.int32, (SLICE, PROBES), 0) + group * SLICE,
        1.0,
        0.0,
    ).astype(BF16)
    arrived(rhs_mid_y, lists_sem.at[1])
    arrived(rhs_root_y, lists_sem.at[2])
    rhs_mid_t = nt(chosen, rhs_mid_y[...].reshape(BLOCK, PROBES))
    rhs_root_t = nt(chosen, rhs_root_y[...].reshape(BLOCK, PROBES))

    mid_pass = pass_on(mid_f, block_sem.at[0], pass_sem.at[0])

    half_rows = pl.ds(pl.multiple_of(half * BLOCK, BLOCK), BLOCK)
    block_rows = pl.ds(pl.multiple_of(y * BLOCK, BLOCK), BLOCK)
    partner = device(x, c, y + 1 - 2 * half, z)
    arrived(terms_in, terms_sem)
    mid_part[...] = -nt(terms_in[...].reshape(2 * SLICE, NZ * COUPLE), places[...])
    mid_part[0:SLICE, half_rows] += rhs_mid_t
    mid_send[...] = mid_part[...].astype(BF16)
    mid_copy = post(mid_send, mid_recv, mid_sem, partner)
    couple_pass = pass_on(couple_f, block_sem.at[1], pass_sem.at[1])
    mid_copy.wait_recv()
    residual_mid = (mid_part[...] + mid_recv[...].astype(F32)).astype(BF16)
    mid_pass.wait_recv()
    forward_mid = join(nt(residual_mid, mid_f[0]), nt(residual_mid, mid_f[1])).astype(BF16)

    def sum_over_y(part, out, into, sem):
        out[...] = part[...].astype(BF16)
        return [
            post(out, into.at[d], sem.at[d], y_mates[d]) for d in range(NY - 1)
        ]

    def total(part, into, copies):
        for copy in copies:
            copy.wait_recv()
        summed = part[...]
        for d in range(NY - 1):
            summed = summed + into[d].astype(F32)
        return summed.astype(BF16)

    couple_pass.wait_recv()
    root_part[...] = -join(nn(forward_mid, couple_f[0]), nn(forward_mid, couple_f[1]))
    root_part[0:SLICE, block_rows] += rhs_root_t
    copies = sum_over_y(root_part, root_send, root_recv, root_sem)
    root_pass = pass_on(root_f, block_sem.at[2], pass_sem.at[2])
    residual_root = total(root_part, root_recv, copies)
    root_pass.wait_recv()
    forward_root = join(nt(residual_root, root_f[0]), nt(residual_root, root_f[1])).astype(BF16)
    root_part[...] = join(nn(forward_root, root_f[0]), nn(forward_root, root_f[1]))
    copies = sum_over_y(root_part, back_send, back_recv, back_sem)
    x_root[...] = total(root_part, back_recv, copies)

    from_root = join(nt(x_root[...], couple_f[0]), nt(x_root[...], couple_f[1]))
    update_mid = (forward_mid.astype(F32) - from_root).astype(BF16)
    mid_part[...] = join(nn(update_mid, mid_f[0]), nn(update_mid, mid_f[1]))
    xmid_send[...] = mid_part[...].astype(BF16)
    xmid_copy = post(xmid_send, xmid_recv, xmid_sem, partner)
    xmid_copy.wait_recv()
    x_mid[...] = (mid_part[...] + xmid_recv[...].astype(F32)).astype(BF16)
    picked_send[...] = nn(x_mid[...], places[...]).astype(BF16).reshape(2, SLICE, NZ * COUPLE)
    for d in range(NZ):
        zl = lax.rem(z + d, NZ)
        post_or_keep(
            picked_send.at[:, :, pl.ds(pl.multiple_of(zl * COUPLE, COUPLE), COUPLE)],
            picked.at[point, :, pl.ds(pl.multiple_of(group * SLICE, SLICE), SLICE), :],
            picked_sem,
            home,
            zl,
        )

    small_send[:, 0:BLOCK] = x_root[:, block_rows]
    small_send[:, BLOCK:] = x_mid[:, half_rows]
    small_copies = [
        post(small_send, small_recv.at[d], small_sem.at[d], x_mates[d]) for d in range(NX - 1)
    ]

    arrived(picked, picked_sem)
    for q in range(2):
        picked_q = picked[q].reshape(2 * PROBES, COUPLE)
        for n in range(2):
            columns = slice(n * 512, (n + 1) * 512)
            change = join(nn(picked_q, couple_v[q, 0, :, columns]), nn(picked_q, couple_v[q, 1, :, columns]))
            live = lax.broadcasted_iota(jnp.int32, change.shape, 1) + n * 512 < size
            update[q, :, columns] = jnp.where(
                live, forward[q, :, columns].astype(F32) - change, 0.0
            ).astype(BF16)

    first = 2 * quad
    sibling = device(x, 1 - c, y, z)

    core_base, chip_base = counter[0], counter[0] + CHUNKS
    counter[0] += CHUNKS + CHUNKS * (NX - 1)

    def core_copy(i):
        return pltpu.make_async_remote_copy(
            src_ref=core_send.at[i],
            dst_ref=core_recv.at[i],
            send_sem=send_sem.at[core_base + i],
            recv_sem=core_sem.at[i],
            device_id=sibling,
            device_id_type=MESH,
        )

    def chip_copy(i, d):
        return pltpu.make_async_remote_copy(
            src_ref=chip_send.at[i, d],
            dst_ref=chip_recv.at[i, d],
            send_sem=send_sem.at[chip_base + i * (NX - 1) + d],
            recv_sem=chip_sem.at[i, d],
            device_id=x_mates[d],
            device_id_type=MESH,
        )

    def leaf_step(i):
        columns = pl.ds(pl.multiple_of(i * CHUNK, CHUNK), CHUNK)
        for q in range(2):
            solved = join(
                nn(update[q], inv_v[q, 0, :, columns]), nn(update[q], inv_v[q, 1, :, columns])
            )
            live = lax.broadcasted_iota(jnp.int32, solved.shape, 1) + i * CHUNK < size
            parts[pl.ds(2 * q * PROBES, 2 * PROBES), :] = jnp.where(live, solved, 0.0)

        def moment(k):
            total_k = None
            for q in range(2):
                for a in range(2):
                    row = (2 * q + a) * PROBES
                    term = weights[first + q, 2 * k + a] * parts[row : row + PROBES, :]
                    total_k = term if total_k is None else total_k + term
            return total_k

        for xx in range(NX):
            core_send[i, xx] = moment(2 * xx + 1 - c).astype(BF16)
            own_sum[i, xx] = moment(2 * xx + c)
        core_copy(i).start()

    def chip_step(i):
        core_copy(i).wait_recv()
        chip_own[i] = own_sum[i, x] + core_recv[i, x].astype(F32)
        for d in range(NX - 1):
            xx = lax.rem(x + d + 1, NX)
            chip_send[i, d] = (own_sum[i, xx] + core_recv[i, xx].astype(F32)).astype(BF16)
            chip_copy(i, d).start()

    def tail_step(i, carry):
        leaf_step(i)

        @pl.when(i > 0)
        def _():
            chip_step(i - 1)

        return carry

    lax.fori_loop(0, CHUNKS, tail_step, 0)
    chip_step(CHUNKS - 1)

    for copy in small_copies:
        copy.wait_recv()
    hosted = lax.div(z, 2)
    pieces = [small_send[...].astype(F32)] + [small_recv[d].astype(F32) for d in range(NX - 1)]
    spread[...] = jnp.zeros_like(spread)
    for cc in range(NC):
        total_k = None
        for d in range(NX):
            point_d = 4 * lax.rem(x + NX - d, NX) + hosted
            real = weights[point_d, 2 * (2 * x + cc)] * pieces[d][0:SLICE]
            imag = weights[point_d, 2 * (2 * x + cc) + 1] * pieces[d][SLICE:]
            total_k = real + imag if total_k is None else total_k + (real + imag)
        spread[pl.ds(pl.multiple_of(group * SLICE, SLICE), SLICE), :] = total_k
        rows_send[cc] = spread[...].T.astype(BF16).reshape(2, BLOCK, PROBES)
    for i in range(NC * NZ):
        place = lax.rem(c * NZ + z + i, NC * NZ)
        cc, zz = lax.div(place, NZ), lax.rem(place, NZ)
        src = rows_send.at[cc, :, pl.ds(pl.multiple_of(zz * OWN, OWN), OWN), :]
        dst = rows_recv.at[i]
        if i == 0:
            pltpu.make_async_copy(src, dst, rows_sem).start()
        else:
            post(src, dst, rows_sem, device(x, cc, y, zz))
    arrived(rows_recv, rows_sem)
    gathered = rows_recv[0].astype(F32)
    for i in range(1, NC * NZ):
        gathered = gathered + rows_recv[i].astype(F32)
    out_root[0] = gathered[0]
    out_mid[0] = gathered[1]

    for i in range(CHUNKS):
        result = chip_own[i]
        for d in range(NX - 1):
            chip_copy(i, d).wait_recv()
            result = result + chip_recv[i, d].astype(F32)
        out_leaf[0, i * CHUNK : (i + 1) * CHUNK, :] = result.T

    for mine, copy in sends:
        if mine is None:
            copy.wait_send()
        else:

            @pl.when(jnp.logical_not(mine))
            def _():
                copy.wait_send()

    for i in range(CHUNKS):
        core_copy(i).wait_send()
        for d in range(NX - 1):
            chip_copy(i, d).wait_send()


def weight_table():
    table = np.zeros((QPOINTS, 2 * MOMENTS), np.float32)
    for q in range(QPOINTS):
        for k in range(MOMENTS):
            angle = 2.0 * math.pi * (q + 0.5) / QPOINTS * (k + 1)
            table[q, 2 * k] = 4.0 / QPOINTS * math.cos(angle)
            table[q, 2 * k + 1] = -4.0 / QPOINTS * math.sin(angle)
    return jnp.asarray(table)


def body(*arrays):
    vmem = pl.BlockSpec(memory_space=pltpu.VMEM)
    smem = pl.BlockSpec(memory_space=pltpu.SMEM)
    hbm = pl.BlockSpec(memory_space=pl.ANY)
    in_specs = [vmem, vmem, vmem, hbm, hbm, vmem, smem, hbm, hbm, hbm, smem]
    out_shape = [
        jax.ShapeDtypeStruct((1, LEAF, PROBES), F32),
        jax.ShapeDtypeStruct((1, OWN, PROBES), F32),
        jax.ShapeDtypeStruct((1, OWN, PROBES), F32),
    ]
    cols = 2 * SLICE
    dma = pltpu.SemaphoreType.DMA
    scratch = [
        pltpu.VMEM((2, 2, LEAF, LEAF), BF16),
        pltpu.VMEM((2, 2, COUPLE, LEAF), BF16),
        pltpu.VMEM((PROBES, LEAF), BF16),
        pltpu.VMEM((2, 2 * PROBES, LEAF), BF16),
        pltpu.VMEM((2, 2 * PROBES, LEAF), BF16),
        pltpu.VMEM((2, BLOCK, SEP), BF16),
        pltpu.VMEM((2, BLOCK, ROOT), BF16),
        pltpu.VMEM((2, BLOCK, ROOT), BF16),
        pltpu.VMEM((SEP, NZ * COUPLE), BF16),
        pltpu.VMEM((NZ, 1, COUPLE), jnp.int32),
        pltpu.VMEM((NZ, OWN, PROBES), BF16),
        pltpu.VMEM((NZ, OWN, PROBES), BF16),
        pltpu.VMEM((2, 2, PROBES, COUPLE), BF16),
        pltpu.VMEM((2, SLICE, NZ * COUPLE), BF16),
        pltpu.VMEM((cols, SEP), F32),
        pltpu.VMEM((cols, SEP), BF16),
        pltpu.VMEM((cols, SEP), BF16),
        pltpu.VMEM((cols, ROOT), F32),
        pltpu.VMEM((cols, ROOT), BF16),
        pltpu.VMEM((NY - 1, cols, ROOT), BF16),
        pltpu.VMEM((cols, ROOT), BF16),
        pltpu.VMEM((NY - 1, cols, ROOT), BF16),
        pltpu.VMEM((cols, ROOT), BF16),
        pltpu.VMEM((cols, SEP), BF16),
        pltpu.VMEM((cols, SEP), BF16),
        pltpu.VMEM((cols, SEP), BF16),
        pltpu.VMEM((2, SLICE, NZ * COUPLE), BF16),
        pltpu.VMEM((2, 2, PROBES, COUPLE), BF16),
        pltpu.VMEM((4 * PROBES, CHUNK), F32),
        pltpu.VMEM((CHUNKS, NX, PROBES, CHUNK), F32),
        pltpu.VMEM((CHUNKS, NX, PROBES, CHUNK), BF16),
        pltpu.VMEM((CHUNKS, NX, PROBES, CHUNK), BF16),
        pltpu.VMEM((CHUNKS, PROBES, CHUNK), F32),
        pltpu.VMEM((CHUNKS, NX - 1, PROBES, CHUNK), BF16),
        pltpu.VMEM((CHUNKS, NX - 1, PROBES, CHUNK), BF16),
        pltpu.VMEM((cols, 2 * BLOCK), BF16),
        pltpu.VMEM((NX - 1, cols, 2 * BLOCK), BF16),
        pltpu.VMEM((PROBES, 2 * BLOCK), F32),
        pltpu.VMEM((NC, 2, BLOCK, PROBES), BF16),
        pltpu.VMEM((NC * NZ, 2, OWN, PROBES), BF16),
        dma((16,)),
        dma,
        dma((3,)),
        dma((3,)),
        dma((3,)),
        dma,
        dma,
        dma((NY - 1,)),
        dma((NY - 1,)),
        dma,
        dma,
        dma((CHUNKS,)),
        dma((CHUNKS, NX - 1)),
        dma((NX - 1,)),
        dma,
        dma((128,)),
    ]
    results = pl.pallas_call(
        kernel,
        out_shape=out_shape,
        in_specs=in_specs,
        out_specs=[vmem, vmem, vmem],
        scratch_shapes=scratch,
        compiler_params=pltpu.CompilerParams(
            collective_id=0, has_side_effects=True, vmem_limit_bytes=48 * 2**20
        ),
    )(*arrays, weight_table())
    return tuple(results)


def solution(mesh):
    in_specs = (
        P("leaf", None),
        P("leaf", None),
        P("leaf", None),
        P("quad", None, "leaf", None),
        P("quad", None, "leaf", None),
        P("leaf", None),
        P("leaf"),
        P("quad", None, "leaf", None),
        P("quad", None, "leaf", None),
        P("quad", None, "leaf", None),
    )
    out_specs = (P("quad", "leaf", None), P("quad", "leaf", None), P("quad", "leaf", None))
    return jax.shard_map(body, mesh=mesh, in_specs=in_specs, out_specs=out_specs, check_vma=False)
```

```python
import functools
import math

import jax
import jax.numpy as jnp
import numpy as np
from jax import lax
from jax.experimental import pallas as pl
from jax.experimental.pallas import tpu as pltpu
from jax.sharding import PartitionSpec as P

MESH = pl.DeviceIdType.MESH
BF16 = jnp.bfloat16
F32 = jnp.float32

MOMENTS = 8
QPOINTS = 16
PROBES = 128
LEAF = 1024
COUPLE = 128
SEP = 512
ROOT = 1024
NX, NY, NZ, NC = 4, 4, 8, 2
OWN = 32
BLOCK = OWN * NZ
SLICE = 32
SHARED = 2 * OWN + 16
CHUNK = 256
CHUNKS = LEAF // CHUNK


def nt(left, right):
    return lax.dot_general(left, right, (((1,), (1,)), ((), ())), preferred_element_type=F32)


def nn(left, right):
    return lax.dot_general(left, right, (((1,), (0,)), ((), ())), preferred_element_type=F32)


def join(with_real, with_imag):
    half = with_real.shape[0] // 2
    return jnp.concatenate(
        [with_real[:half] - with_imag[half:], with_real[half:] + with_imag[:half]], axis=0
    )


def kernel(
    rhs_leaf_h,
    rhs_mid,
    rhs_root,
    leaf_inv,
    leaf_couple,
    row_list,
    leaf_size_h,
    mid_inv,
    mid_root,
    root_inv,
    weights_h,
    out_leaf,
    out_mid,
    out_root,
    rhs_leaf,
    leaf_size,
    weights,
    inv_v,
    couple_v,
    source,
    solved_rows,
    forward,
    update,
    mid_f,
    couple_f,
    root_f,
    places,
    list_v,
    shared,
    shared_y,
    terms,
    terms_in,
    mid_part,
    mid_send,
    mid_recv,
    root_part,
    root_send,
    root_recv,
    back_send,
    back_recv,
    x_root,
    xmid_send,
    xmid_recv,
    x_mid,
    picked_send,
    picked,
    parts,
    own_sum,
    core_send,
    core_recv,
    chip_own,
    chip_send,
    chip_recv,
    small_send,
    small_recv,
    spread,
    rows_send,
    rows_recv,
    load_sem,
    inv_sem,
    couple_sem,
    shared_sem,
    block_sem,
    relay_sem,
    pass_sem,
    terms_sem,
    mid_sem,
    root_sem,
    back_sem,
    xmid_sem,
    picked_sem,
    core_sem,
    chip_sem,
    small_sem,
    rows_sem,
    send_sem,
):
    quad, leaf = lax.axis_index("quad"), lax.axis_index("leaf")
    x, c = lax.div(quad, 2), lax.rem(quad, 2)
    y, z = lax.div(leaf, NZ), lax.rem(leaf, NZ)
    home = lax.div(z, 4)
    point = lax.rem(lax.div(z, 2), 2)
    group = 2 * lax.rem(z, 2) + c
    half = lax.rem(y, 2)
    sends = []
    counter = [0]

    def device(xx, cc, yy, zz):
        return (2 * xx + cc, NZ * yy + zz)

    def send(src, dst, recv, target):
        copy = pltpu.make_async_remote_copy(
            src_ref=src,
            dst_ref=dst,
            send_sem=send_sem.at[counter[0]],
            recv_sem=recv,
            device_id=target,
            device_id_type=MESH,
        )
        counter[0] += 1
        return copy

    def post(src, dst, recv, target):
        copy = send(src, dst, recv, target)
        copy.start()
        sends.append((None, copy))
        return copy

    def post_or_keep(src, dst, recv, cc, zz):
        mine = jnp.logical_and(cc == c, zz == z)
        copy = send(src, dst, recv, device(x, cc, y, zz))

        @pl.when(mine)
        def _():
            pltpu.make_async_copy(src, dst, recv).start()

        @pl.when(jnp.logical_not(mine))
        def _():
            copy.start()

        sends.append((mine, copy))

    def arrived(buffer, sem):
        pltpu.make_async_copy(buffer, buffer, sem).wait()

    def spread_blocks(k):
        matrix, whole, columns = pieces[k]
        for q in range(2):
            slot = lax.rem(z - 2 * (2 * c + q) + 3 + NZ, NZ)
            near = 2 * (2 * c + q) + lax.div(slot, 4)
            for cc in range(NC):
                post_or_keep(
                    matrix.at[q, cc, :, columns],
                    whole.at[cc, pl.ds(pl.multiple_of(slot * OWN, OWN), OWN), columns],
                    block_sem.at[k],
                    cc,
                    near,
                )

    first_half, second_half = pl.ds(0, ROOT // 2), pl.ds(ROOT // 2, ROOT // 2)
    pieces = (
        (mid_inv, mid_f, pl.ds(0, SEP)),
        (mid_root, couple_f, first_half),
        (mid_root, couple_f, second_half),
        (root_inv, root_f, first_half),
        (root_inv, root_f, second_half),
    )
    side = lax.rem(z, 2)
    pair = device(x, c, y, z + 1 - 2 * side)
    sibling = device(x, 1 - c, y, z)
    near_rows = pl.ds(pl.multiple_of(side * (BLOCK // 2), BLOCK // 2), BLOCK // 2)
    far_rows = pl.ds(pl.multiple_of((1 - side) * (BLOCK // 2), BLOCK // 2), BLOCK // 2)

    def relay(k):
        rows = pieces[k][1].at[c, near_rows, pieces[k][2]]
        arrived(rows, block_sem.at[k])
        return [
            post(rows, rows, relay_sem.at[k], pair),
            post(rows, rows, pass_sem.at[k, 0], sibling),
        ]

    def pass_far(k, copies):
        copies[0].wait_recv()
        rows = pieces[k][1].at[c, far_rows, pieces[k][2]]
        copies.append(post(rows, rows, pass_sem.at[k, 1], sibling))

    def complete(copies):
        copies[1].wait_recv()
        copies[2].wait_recv()

    loads = [
        pltpu.make_async_copy(leaf_size_h, leaf_size, load_sem.at[0]),
        pltpu.make_async_copy(rhs_leaf_h, rhs_leaf, load_sem.at[1]),
        pltpu.make_async_copy(weights_h, weights, load_sem.at[2]),
        pltpu.make_async_copy(row_list, list_v, load_sem.at[3]),
        pltpu.make_async_copy(rhs_mid, shared.at[pl.ds(0, OWN)], load_sem.at[4]),
        pltpu.make_async_copy(rhs_root, shared.at[pl.ds(OWN, OWN)], load_sem.at[5]),
    ]
    for load in loads:
        load.start()
    for i in range(4):
        block = (i // 2, i % 2)
        pltpu.make_async_copy(leaf_inv.at[block], inv_v.at[block], inv_sem.at[i]).start()
    couple_load = pltpu.make_async_copy(leaf_couple, couple_v, couple_sem)
    couple_load.start()

    barrier = pltpu.get_barrier_semaphore()
    mates = []
    for i in range(1, NC * NZ):
        place = lax.rem(c * NZ + z + i, NC * NZ)
        mates.append(device(x, lax.div(place, NZ), y, lax.rem(place, NZ)))
    y_mates = [device(x, c, lax.rem(y + d, NY), z) for d in range(1, NY)]
    x_mates = [device(lax.rem(x + d, NX), c, y, z) for d in range(1, NX)]
    for mate in mates + y_mates + x_mates:
        pl.semaphore_signal(barrier, inc=1, device_id=mate, device_id_type=MESH)

    for load in loads:
        load.wait()
    size = leaf_size[0]
    listed = jnp.broadcast_to(list_v[...], (16, COUPLE))
    high = lax.div(listed, 16)
    low = listed - 16 * high
    first_row = lax.broadcasted_iota(jnp.int32, (16, COUPLE), 0) == 0
    shared[2 * OWN : SHARED, :] = jnp.where(first_row, high, low).astype(F32).astype(BF16)
    row_live = lax.broadcasted_iota(jnp.int32, (LEAF, PROBES), 0) < size
    source[...] = jnp.where(row_live, rhs_leaf[...].astype(F32), 0.0).astype(BF16)

    def forward_step(i, carry):
        q, a = lax.div(i, 2), lax.rem(i, 2)
        arrived(inv_v.at[q, a], inv_sem.at[i])
        product = nn(inv_v[q, a], source[...])
        live = lax.broadcasted_iota(jnp.int32, product.shape, 0) < size
        solved_rows[q, :, pl.ds(pl.multiple_of(a * PROBES, PROBES), PROBES)] = jnp.where(
            live, product, 0.0
        ).astype(BF16)
        return carry

    def couple_step(q):
        with_real = nn(couple_v[q, 0], solved_rows[q])
        with_imag = nn(couple_v[q, 1], solved_rows[q])
        terms[q, 0] = (with_real[:, :PROBES] - with_imag[:, PROBES:]).T.astype(BF16)
        terms[q, 1] = (with_real[:, PROBES:] + with_imag[:, :PROBES]).T.astype(BF16)

    def terms_out(q):
        for t in (2 * q, 2 * q + 1):
            for cc in range(NC):
                pg = 2 * (t % 2) + cc
                post_or_keep(
                    terms.at[q, :, pl.ds(pg * SLICE, SLICE), :],
                    terms_in.at[:, :, pl.ds(pl.multiple_of(z * COUPLE, COUPLE), COUPLE)],
                    terms_sem,
                    cc,
                    4 * c + t,
                )

    lax.fori_loop(0, 4, forward_step, 0)
    couple_load.wait()
    couple_step(0)
    couple_step(1)
    pl.semaphore_wait(barrier, len(mates) + len(y_mates) + len(x_mates))

    spread_blocks(1)
    spread_blocks(2)
    spread_blocks(0)
    terms_out(0)
    terms_out(1)
    pltpu.make_async_copy(shared, shared_y.at[z], shared_sem).start()
    for d in range(1, NZ):
        post(shared, shared_y.at[z], shared_sem, device(x, c, y, lax.rem(z + d, NZ)))

    couple_copies = [relay(1), relay(2)]
    spread_blocks(3)
    spread_blocks(4)
    mid_copies = relay(0)
    arrived(shared_y, shared_sem)
    for l in range(NZ):
        sep_row = lax.broadcasted_iota(jnp.int32, (SEP, COUPLE), 0)
        codes = shared_y[l, 2 * OWN : SHARED, :].astype(F32)
        listed = (16.0 * codes[0:1] + codes[1:2]).astype(jnp.int32)
        places[:, l * COUPLE : (l + 1) * COUPLE] = (
            jnp.where(sep_row == listed, 1.0, 0.0).astype(BF16)
        )
    chosen = jnp.where(
        lax.broadcasted_iota(jnp.int32, (SLICE, PROBES), 1)
        == lax.broadcasted_iota(jnp.int32, (SLICE, PROBES), 0) + group * SLICE,
        1.0,
        0.0,
    ).astype(BF16)
    rhs_mid_t = nt(chosen, shared_y[:, 0:OWN, :].reshape(BLOCK, PROBES))
    rhs_root_t = nt(chosen, shared_y[:, OWN : 2 * OWN, :].reshape(BLOCK, PROBES))

    for q in range(2):
        forward[q] = solved_rows[q].T

    half_rows = pl.ds(pl.multiple_of(half * BLOCK, BLOCK), BLOCK)
    block_rows = pl.ds(pl.multiple_of(y * BLOCK, BLOCK), BLOCK)
    partner = device(x, c, y + 1 - 2 * half, z)
    arrived(terms_in, terms_sem)
    mid_part[...] = -nt(terms_in[...].reshape(2 * SLICE, NZ * COUPLE), places[...])
    mid_part[0:SLICE, half_rows] += rhs_mid_t
    mid_send[...] = mid_part[...].astype(BF16)
    mid_copy = post(mid_send, mid_recv, mid_sem, partner)
    pass_far(1, couple_copies[0])
    pass_far(2, couple_copies[1])
    pass_far(0, mid_copies)
    mid_copy.wait_recv()
    residual_mid = (mid_part[...] + mid_recv[...].astype(F32)).astype(BF16)
    complete(mid_copies)
    forward_mid = join(nt(residual_mid, mid_f[0]), nt(residual_mid, mid_f[1])).astype(BF16)

    def sum_over_y(part, out, into, sem):
        out[...] = part[...].astype(BF16)
        return [
            post(out, into.at[d], sem.at[d], y_mates[d]) for d in range(NY - 1)
        ]

    def total(part, into, copies):
        for copy in copies:
            copy.wait_recv()
        summed = part[...]
        for d in range(NY - 1):
            summed = summed + into[d].astype(F32)
        return summed.astype(BF16)

    complete(couple_copies[0])
    complete(couple_copies[1])
    root_part[...] = -join(nn(forward_mid, couple_f[0]), nn(forward_mid, couple_f[1]))
    root_part[0:SLICE, block_rows] += rhs_root_t
    copies = sum_over_y(root_part, root_send, root_recv, root_sem)
    root_copies = [relay(3), relay(4)]
    pass_far(3, root_copies[0])
    pass_far(4, root_copies[1])
    residual_root = total(root_part, root_recv, copies)
    complete(root_copies[0])
    complete(root_copies[1])
    forward_root = join(nt(residual_root, root_f[0]), nt(residual_root, root_f[1])).astype(BF16)
    root_part[...] = join(nn(forward_root, root_f[0]), nn(forward_root, root_f[1]))
    copies = sum_over_y(root_part, back_send, back_recv, back_sem)
    x_root[...] = total(root_part, back_recv, copies)

    from_root = join(nt(x_root[...], couple_f[0]), nt(x_root[...], couple_f[1]))
    update_mid = (forward_mid.astype(F32) - from_root).astype(BF16)
    mid_part[...] = join(nn(update_mid, mid_f[0]), nn(update_mid, mid_f[1]))
    xmid_send[...] = mid_part[...].astype(BF16)
    xmid_copy = post(xmid_send, xmid_recv, xmid_sem, partner)
    xmid_copy.wait_recv()
    x_mid[...] = (mid_part[...] + xmid_recv[...].astype(F32)).astype(BF16)
    picked_send[...] = nn(x_mid[...], places[...]).astype(BF16).reshape(2, SLICE, NZ * COUPLE)
    for d in range(NZ):
        zl = lax.rem(z + d, NZ)
        post_or_keep(
            picked_send.at[:, :, pl.ds(pl.multiple_of(zl * COUPLE, COUPLE), COUPLE)],
            picked.at[point, :, pl.ds(pl.multiple_of(group * SLICE, SLICE), SLICE), :],
            picked_sem,
            home,
            zl,
        )

    small_send[:, 0:BLOCK] = x_root[:, block_rows]
    small_send[:, BLOCK:] = x_mid[:, half_rows]
    small_copies = [
        post(small_send, small_recv.at[d], small_sem.at[d], x_mates[d]) for d in range(NX - 1)
    ]

    arrived(picked, picked_sem)
    for q in range(2):
        picked_q = picked[q].reshape(2 * PROBES, COUPLE)
        for n in range(2):
            columns = slice(n * 512, (n + 1) * 512)
            change = join(nn(picked_q, couple_v[q, 0, :, columns]), nn(picked_q, couple_v[q, 1, :, columns]))
            live = lax.broadcasted_iota(jnp.int32, change.shape, 1) + n * 512 < size
            update[q, :, columns] = jnp.where(
                live, forward[q, :, columns].astype(F32) - change, 0.0
            ).astype(BF16)

    first = 2 * quad

    core_base, chip_base = counter[0], counter[0] + CHUNKS
    counter[0] += CHUNKS + CHUNKS * (NX - 1)

    def core_copy(i):
        return pltpu.make_async_remote_copy(
            src_ref=core_send.at[i],
            dst_ref=core_recv.at[i],
            send_sem=send_sem.at[core_base + i],
            recv_sem=core_sem.at[i],
            device_id=sibling,
            device_id_type=MESH,
        )

    def chip_copy(i, d):
        return pltpu.make_async_remote_copy(
            src_ref=chip_send.at[i, d],
            dst_ref=chip_recv.at[i, d],
            send_sem=send_sem.at[chip_base + i * (NX - 1) + d],
            recv_sem=chip_sem.at[i, d],
            device_id=x_mates[d],
            device_id_type=MESH,
        )

    def leaf_step(i):
        columns = pl.ds(pl.multiple_of(i * CHUNK, CHUNK), CHUNK)
        for q in range(2):
            solved = join(
                nn(update[q], inv_v[q, 0, :, columns]), nn(update[q], inv_v[q, 1, :, columns])
            )
            live = lax.broadcasted_iota(jnp.int32, solved.shape, 1) + i * CHUNK < size
            parts[pl.ds(2 * q * PROBES, 2 * PROBES), :] = jnp.where(live, solved, 0.0)

        def moment(k):
            total_k = None
            for q in range(2):
                for a in range(2):
                    row = (2 * q + a) * PROBES
                    term = weights[first + q, 2 * k + a] * parts[row : row + PROBES, :]
                    total_k = term if total_k is None else total_k + term
            return total_k

        for xx in range(NX):
            core_send[i, xx] = moment(2 * xx + 1 - c).astype(BF16)
            own_sum[i, xx] = moment(2 * xx + c)
        core_copy(i).start()

    def chip_step(i):
        core_copy(i).wait_recv()
        chip_own[i] = own_sum[i, x] + core_recv[i, x].astype(F32)
        for d in range(NX - 1):
            xx = lax.rem(x + d + 1, NX)
            chip_send[i, d] = (own_sum[i, xx] + core_recv[i, xx].astype(F32)).astype(BF16)
            chip_copy(i, d).start()

    def tail_step(i, carry):
        leaf_step(i)

        @pl.when(i > 0)
        def _():
            chip_step(i - 1)

        return carry

    lax.fori_loop(0, CHUNKS, tail_step, 0)
    chip_step(CHUNKS - 1)

    for copy in small_copies:
        copy.wait_recv()
    hosted = lax.div(z, 2)
    pieces = [small_send[...].astype(F32)] + [small_recv[d].astype(F32) for d in range(NX - 1)]
    spread[...] = jnp.zeros_like(spread)
    for cc in range(NC):
        total_k = None
        for d in range(NX):
            point_d = 4 * lax.rem(x + NX - d, NX) + hosted
            real = weights[point_d, 2 * (2 * x + cc)] * pieces[d][0:SLICE]
            imag = weights[point_d, 2 * (2 * x + cc) + 1] * pieces[d][SLICE:]
            total_k = real + imag if total_k is None else total_k + (real + imag)
        spread[pl.ds(pl.multiple_of(group * SLICE, SLICE), SLICE), :] = total_k
        rows_send[cc] = spread[...].T.astype(BF16).reshape(2, BLOCK, PROBES)
    for i in range(NC * NZ):
        place = lax.rem(c * NZ + z + i, NC * NZ)
        cc, zz = lax.div(place, NZ), lax.rem(place, NZ)
        src = rows_send.at[cc, :, pl.ds(pl.multiple_of(zz * OWN, OWN), OWN), :]
        dst = rows_recv.at[i]
        if i == 0:
            pltpu.make_async_copy(src, dst, rows_sem).start()
        else:
            post(src, dst, rows_sem, device(x, cc, y, zz))
    arrived(rows_recv, rows_sem)
    gathered = rows_recv[0].astype(F32)
    for i in range(1, NC * NZ):
        gathered = gathered + rows_recv[i].astype(F32)
    out_root[0] = gathered[0]
    out_mid[0] = gathered[1]

    for i in range(CHUNKS):
        result = chip_own[i]
        for d in range(NX - 1):
            chip_copy(i, d).wait_recv()
            result = result + chip_recv[i, d].astype(F32)
        out_leaf[0, i * CHUNK : (i + 1) * CHUNK, :] = result.T

    for mine, copy in sends:
        if mine is None:
            copy.wait_send()
        else:

            @pl.when(jnp.logical_not(mine))
            def _():
                copy.wait_send()

    for i in range(CHUNKS):
        core_copy(i).wait_send()
        for d in range(NX - 1):
            chip_copy(i, d).wait_send()


def deliver(leaf, mid, root, out_leaf, out_mid, out_root):
    out_leaf[...] = leaf[...]
    out_mid[...] = mid[...]
    out_root[...] = root[...]


def weight_table():
    table = np.zeros((QPOINTS, 2 * MOMENTS), np.float32)
    for q in range(QPOINTS):
        for k in range(MOMENTS):
            angle = 2.0 * math.pi * (q + 0.5) / QPOINTS * (k + 1)
            table[q, 2 * k] = 4.0 / QPOINTS * math.cos(angle)
            table[q, 2 * k + 1] = -4.0 / QPOINTS * math.sin(angle)
    return jnp.asarray(table)


def body(*arrays):
    vmem = pl.BlockSpec(memory_space=pltpu.VMEM)
    hbm = pl.BlockSpec(memory_space=pltpu.HBM)
    in_specs = [hbm] * 11
    out_shape = [
        jax.ShapeDtypeStruct((1, LEAF, PROBES), F32),
        jax.ShapeDtypeStruct((1, OWN, PROBES), F32),
        jax.ShapeDtypeStruct((1, OWN, PROBES), F32),
    ]
    cols = 2 * SLICE
    dma = pltpu.SemaphoreType.DMA
    scratch = [
        pltpu.VMEM((LEAF, PROBES), BF16),
        pltpu.SMEM((1,), jnp.int32),
        pltpu.SMEM((QPOINTS, 2 * MOMENTS), F32),
        pltpu.VMEM((2, 2, LEAF, LEAF), BF16),
        pltpu.VMEM((2, 2, COUPLE, LEAF), BF16),
        pltpu.VMEM((LEAF, PROBES), BF16),
        pltpu.VMEM((2, LEAF, 2 * PROBES), BF16),
        pltpu.VMEM((2, 2 * PROBES, LEAF), BF16),
        pltpu.VMEM((2, 2 * PROBES, LEAF), BF16),
        pltpu.VMEM((2, BLOCK, SEP), BF16),
        pltpu.VMEM((2, BLOCK, ROOT), BF16),
        pltpu.VMEM((2, BLOCK, ROOT), BF16),
        pltpu.VMEM((SEP, NZ * COUPLE), BF16),
        pltpu.VMEM((1, COUPLE), jnp.int32),
        pltpu.VMEM((SHARED, PROBES), BF16),
        pltpu.VMEM((NZ, SHARED, PROBES), BF16),
        pltpu.VMEM((2, 2, PROBES, COUPLE), BF16),
        pltpu.VMEM((2, SLICE, NZ * COUPLE), BF16),
        pltpu.VMEM((cols, SEP), F32),
        pltpu.VMEM((cols, SEP), BF16),
        pltpu.VMEM((cols, SEP), BF16),
        pltpu.VMEM((cols, ROOT), F32),
        pltpu.VMEM((cols, ROOT), BF16),
        pltpu.VMEM((NY - 1, cols, ROOT), BF16),
        pltpu.VMEM((cols, ROOT), BF16),
        pltpu.VMEM((NY - 1, cols, ROOT), BF16),
        pltpu.VMEM((cols, ROOT), BF16),
        pltpu.VMEM((cols, SEP), BF16),
        pltpu.VMEM((cols, SEP), BF16),
        pltpu.VMEM((cols, SEP), BF16),
        pltpu.VMEM((2, SLICE, NZ * COUPLE), BF16),
        pltpu.VMEM((2, 2, PROBES, COUPLE), BF16),
        pltpu.VMEM((4 * PROBES, CHUNK), F32),
        pltpu.VMEM((CHUNKS, NX, PROBES, CHUNK), F32),
        pltpu.VMEM((CHUNKS, NX, PROBES, CHUNK), BF16),
        pltpu.VMEM((CHUNKS, NX, PROBES, CHUNK), BF16),
        pltpu.VMEM((CHUNKS, PROBES, CHUNK), F32),
        pltpu.VMEM((CHUNKS, NX - 1, PROBES, CHUNK), BF16),
        pltpu.VMEM((CHUNKS, NX - 1, PROBES, CHUNK), BF16),
        pltpu.VMEM((cols, 2 * BLOCK), BF16),
        pltpu.VMEM((NX - 1, cols, 2 * BLOCK), BF16),
        pltpu.VMEM((PROBES, 2 * BLOCK), F32),
        pltpu.VMEM((NC, 2, BLOCK, PROBES), BF16),
        pltpu.VMEM((NC * NZ, 2, OWN, PROBES), BF16),
        dma((6,)),
        dma((4,)),
        dma,
        dma,
        dma((5,)),
        dma((5,)),
        dma((5, 2)),
        dma,
        dma,
        dma((NY - 1,)),
        dma((NY - 1,)),
        dma,
        dma,
        dma((CHUNKS,)),
        dma((CHUNKS, NX - 1)),
        dma((NX - 1,)),
        dma,
        dma((128,)),
    ]
    results = pl.pallas_call(
        kernel,
        out_shape=out_shape,
        in_specs=in_specs,
        out_specs=[vmem, vmem, vmem],
        scratch_shapes=scratch,
        compiler_params=pltpu.CompilerParams(
            collective_id=0, has_side_effects=True, vmem_limit_bytes=56 * 2**20
        ),
    )(*arrays, weight_table())
    return tuple(
        pl.pallas_call(
            deliver,
            out_shape=out_shape,
            in_specs=[vmem] * 3,
            out_specs=[vmem] * 3,
        )(*results)
    )


def solution(mesh):
    in_specs = (
        P("leaf", None),
        P("leaf", None),
        P("leaf", None),
        P("quad", None, "leaf", None),
        P("quad", None, "leaf", None),
        P("leaf", None),
        P("leaf"),
        P("quad", None, "leaf", None),
        P("quad", None, "leaf", None),
        P("quad", None, "leaf", None),
    )
    out_specs = (P("quad", "leaf", None), P("quad", "leaf", None), P("quad", "leaf", None))
    return jax.shard_map(body, mesh=mesh, in_specs=in_specs, out_specs=out_specs, check_vma=False)
```

```python
import functools
import math

import jax
import jax.numpy as jnp
import numpy as np
from jax import lax
from jax.experimental import pallas as pl
from jax.experimental.pallas import tpu as pltpu
from jax.sharding import PartitionSpec as P

MESH = pl.DeviceIdType.MESH
BF16 = jnp.bfloat16
F32 = jnp.float32

MOMENTS = 8
QPOINTS = 16
PROBES = 128
LEAF = 1024
COUPLE = 128
SEP = 512
ROOT = 1024
NX, NY, NZ, NC = 4, 4, 8, 2
OWN = 32
BLOCK = OWN * NZ
SLICE = 32
SHARED = OWN + 16
CHUNK = 256
CHUNKS = LEAF // CHUNK


def nt(left, right):
    return lax.dot_general(left, right, (((1,), (1,)), ((), ())), preferred_element_type=F32)


def nn(left, right):
    return lax.dot_general(left, right, (((1,), (0,)), ((), ())), preferred_element_type=F32)


def join(with_real, with_imag):
    half = with_real.shape[0] // 2
    return jnp.concatenate(
        [with_real[:half] - with_imag[half:], with_real[half:] + with_imag[:half]], axis=0
    )


def kernel(
    rhs_leaf_h,
    rhs_mid,
    rhs_root,
    leaf_inv,
    leaf_couple,
    row_list,
    leaf_size_h,
    mid_inv,
    mid_root,
    root_inv,
    weights_h,
    out_leaf,
    out_mid,
    out_root,
    rhs_leaf,
    leaf_size,
    weights,
    inv_v,
    couple_v,
    source,
    solved_rows,
    forward,
    update,
    mid_f,
    couple_f,
    root_f,
    places,
    list_v,
    shared,
    shared_y,
    other_y,
    terms,
    terms_in,
    mid_part,
    mid_send,
    mid_recv,
    root_part,
    root_send,
    root_recv,
    back_send,
    back_recv,
    x_root,
    xmid_send,
    xmid_recv,
    x_mid,
    picked_send,
    picked,
    parts,
    own_sum,
    core_send,
    core_recv,
    chip_own,
    chip_send,
    chip_recv,
    small_send,
    small_recv,
    spread,
    rows_send,
    rows_recv,
    load_sem,
    inv_sem,
    couple_sem,
    shared_sem,
    other_sem,
    block_sem,
    relay_sem,
    pass_sem,
    terms_sem,
    mid_sem,
    root_sem,
    back_sem,
    xmid_sem,
    picked_sem,
    core_sem,
    chip_sem,
    small_sem,
    rows_sem,
    send_sem,
):
    quad, leaf = lax.axis_index("quad"), lax.axis_index("leaf")
    x, c = lax.div(quad, 2), lax.rem(quad, 2)
    y, z = lax.div(leaf, NZ), lax.rem(leaf, NZ)
    home = lax.div(z, 4)
    point = lax.rem(lax.div(z, 2), 2)
    group = 2 * lax.rem(z, 2) + c
    half = lax.rem(y, 2)
    sends = []
    counter = [0]

    def device(xx, cc, yy, zz):
        return (2 * xx + cc, NZ * yy + zz)

    def send(src, dst, recv, target):
        copy = pltpu.make_async_remote_copy(
            src_ref=src,
            dst_ref=dst,
            send_sem=send_sem.at[counter[0]],
            recv_sem=recv,
            device_id=target,
            device_id_type=MESH,
        )
        counter[0] += 1
        return copy

    def post(src, dst, recv, target):
        copy = send(src, dst, recv, target)
        copy.start()
        sends.append((None, copy))
        return copy

    def post_or_keep(src, dst, recv, cc, zz):
        mine = jnp.logical_and(cc == c, zz == z)
        copy = send(src, dst, recv, device(x, cc, y, zz))

        @pl.when(mine)
        def _():
            pltpu.make_async_copy(src, dst, recv).start()

        @pl.when(jnp.logical_not(mine))
        def _():
            copy.start()

        sends.append((mine, copy))

    def arrived(buffer, sem):
        pltpu.make_async_copy(buffer, buffer, sem).wait()

    def spread_blocks(k):
        matrix, whole, columns = pieces[k]
        for q in range(2):
            slot = lax.rem(z - 2 * (2 * c + q) + 3 + NZ, NZ)
            near = 2 * (2 * c + q) + lax.div(slot, 4)
            for cc in range(NC):
                post_or_keep(
                    matrix.at[q, cc, :, columns],
                    whole.at[cc, pl.ds(pl.multiple_of(slot * OWN, OWN), OWN), columns],
                    block_sem.at[k],
                    cc,
                    near,
                )

    first_half, second_half = pl.ds(0, ROOT // 2), pl.ds(ROOT // 2, ROOT // 2)
    pieces = (
        (mid_inv, mid_f, pl.ds(0, SEP)),
        (mid_root, couple_f, first_half),
        (mid_root, couple_f, second_half),
        (root_inv, root_f, first_half),
        (root_inv, root_f, second_half),
    )
    side = lax.rem(z, 2)
    pair = device(x, c, y, z + 1 - 2 * side)
    sibling = device(x, 1 - c, y, z)
    near_rows = pl.ds(pl.multiple_of(side * (BLOCK // 2), BLOCK // 2), BLOCK // 2)
    far_rows = pl.ds(pl.multiple_of((1 - side) * (BLOCK // 2), BLOCK // 2), BLOCK // 2)

    def relay(k):
        rows = pieces[k][1].at[c, near_rows, pieces[k][2]]
        arrived(rows, block_sem.at[k])
        return [
            post(rows, rows, relay_sem.at[k], pair),
            post(rows, rows, pass_sem.at[k, 0], sibling),
        ]

    def pass_far(k, copies):
        copies[0].wait_recv()
        rows = pieces[k][1].at[c, far_rows, pieces[k][2]]
        copies.append(post(rows, rows, pass_sem.at[k, 1], sibling))

    def complete(copies):
        copies[1].wait_recv()
        copies[2].wait_recv()

    loads = [
        pltpu.make_async_copy(leaf_size_h, leaf_size, load_sem.at[0]),
        pltpu.make_async_copy(rhs_leaf_h, rhs_leaf, load_sem.at[1]),
        pltpu.make_async_copy(weights_h, weights, load_sem.at[2]),
        pltpu.make_async_copy(row_list, list_v, load_sem.at[3]),
    ]
    for load in loads:
        load.start()
    mid_load = pltpu.make_async_copy(rhs_mid, shared.at[pl.ds(0, OWN)], load_sem.at[4])
    root_load = pltpu.make_async_copy(rhs_root, shared.at[pl.ds(0, OWN)], load_sem.at[4])

    @pl.when(c == 0)
    def _():
        mid_load.start()

    @pl.when(c == 1)
    def _():
        root_load.start()

    for i in range(4):
        block = (i // 2, i % 2)
        pltpu.make_async_copy(leaf_inv.at[block], inv_v.at[block], inv_sem.at[i]).start()
    couple_load = pltpu.make_async_copy(leaf_couple, couple_v, couple_sem)
    couple_load.start()

    barrier = pltpu.get_barrier_semaphore()
    mates = []
    for i in range(1, NC * NZ):
        place = lax.rem(c * NZ + z + i, NC * NZ)
        mates.append(device(x, lax.div(place, NZ), y, lax.rem(place, NZ)))
    y_mates = [device(x, c, lax.rem(y + d, NY), z) for d in range(1, NY)]
    x_mates = [device(lax.rem(x + d, NX), c, y, z) for d in range(1, NX)]
    for mate in mates + y_mates + x_mates:
        pl.semaphore_signal(barrier, inc=1, device_id=mate, device_id_type=MESH)

    for load in loads:
        load.wait()
    mid_load.wait()
    size = leaf_size[0]
    listed = jnp.broadcast_to(list_v[...], (16, COUPLE))
    high = lax.div(listed, 16)
    low = listed - 16 * high
    first_row = lax.broadcasted_iota(jnp.int32, (16, COUPLE), 0) == 0
    shared[OWN:SHARED, :] = jnp.where(first_row, high, low).astype(F32).astype(BF16)
    row_live = lax.broadcasted_iota(jnp.int32, (LEAF, PROBES), 0) < size
    source[...] = jnp.where(row_live, rhs_leaf[...].astype(F32), 0.0).astype(BF16)

    def forward_step(i, carry):
        q, a = lax.div(i, 2), lax.rem(i, 2)
        arrived(inv_v.at[q, a], inv_sem.at[i])
        product = nn(inv_v[q, a], source[...])
        live = lax.broadcasted_iota(jnp.int32, product.shape, 0) < size
        solved_rows[q, :, pl.ds(pl.multiple_of(a * PROBES, PROBES), PROBES)] = jnp.where(
            live, product, 0.0
        ).astype(BF16)
        return carry

    def couple_step(q):
        with_real = nn(couple_v[q, 0], solved_rows[q])
        with_imag = nn(couple_v[q, 1], solved_rows[q])
        terms[q, 0] = (with_real[:, :PROBES] - with_imag[:, PROBES:]).T.astype(BF16)
        terms[q, 1] = (with_real[:, PROBES:] + with_imag[:, :PROBES]).T.astype(BF16)

    def terms_out(q):
        for t in (2 * q, 2 * q + 1):
            for cc in range(NC):
                pg = 2 * (t % 2) + cc
                post_or_keep(
                    terms.at[q, :, pl.ds(pg * SLICE, SLICE), :],
                    terms_in.at[:, :, pl.ds(pl.multiple_of(z * COUPLE, COUPLE), COUPLE)],
                    terms_sem,
                    cc,
                    4 * c + t,
                )

    lax.fori_loop(0, 4, forward_step, 0)
    couple_load.wait()
    couple_step(0)
    couple_step(1)
    pl.semaphore_wait(barrier, len(mates) + len(y_mates) + len(x_mates))

    spread_blocks(1)
    terms_out(0)
    terms_out(1)
    spread_blocks(2)
    spread_blocks(0)
    pltpu.make_async_copy(shared, shared_y.at[z], shared_sem).start()
    for d in range(1, NZ):
        post(shared, shared_y.at[z], shared_sem, device(x, c, y, lax.rem(z + d, NZ)))

    couple_copies = [relay(1), relay(2)]
    spread_blocks(3)
    spread_blocks(4)
    mid_copies = relay(0)
    arrived(shared_y, shared_sem)
    other_copy = post(shared_y.at[:, pl.ds(0, OWN)], other_y, other_sem, sibling)
    for l in range(NZ):
        sep_row = lax.broadcasted_iota(jnp.int32, (SEP, COUPLE), 0)
        codes = shared_y[l, OWN:SHARED, :].astype(F32)
        listed = (16.0 * codes[0:1] + codes[1:2]).astype(jnp.int32)
        places[:, l * COUPLE : (l + 1) * COUPLE] = (
            jnp.where(sep_row == listed, 1.0, 0.0).astype(BF16)
        )
    chosen = jnp.where(
        lax.broadcasted_iota(jnp.int32, (SLICE, PROBES), 1)
        == lax.broadcasted_iota(jnp.int32, (SLICE, PROBES), 0) + group * SLICE,
        1.0,
        0.0,
    ).astype(BF16)
    other_copy.wait_recv()
    mine_t = nt(chosen, shared_y[:, 0:OWN, :].reshape(BLOCK, PROBES))
    other_t = nt(chosen, other_y[...].reshape(BLOCK, PROBES))
    rhs_mid_t = jnp.where(c == 0, mine_t, other_t)
    rhs_root_t = jnp.where(c == 0, other_t, mine_t)

    for q in range(2):
        forward[q] = solved_rows[q].T

    half_rows = pl.ds(pl.multiple_of(half * BLOCK, BLOCK), BLOCK)
    block_rows = pl.ds(pl.multiple_of(y * BLOCK, BLOCK), BLOCK)
    partner = device(x, c, y + 1 - 2 * half, z)
    arrived(terms_in, terms_sem)
    mid_part[...] = -nt(terms_in[...].reshape(2 * SLICE, NZ * COUPLE), places[...])
    mid_part[0:SLICE, half_rows] += rhs_mid_t
    mid_send[...] = mid_part[...].astype(BF16)
    mid_copy = post(mid_send, mid_recv, mid_sem, partner)
    pass_far(1, couple_copies[0])
    pass_far(2, couple_copies[1])
    pass_far(0, mid_copies)
    mid_copy.wait_recv()
    residual_mid = (mid_part[...] + mid_recv[...].astype(F32)).astype(BF16)
    complete(mid_copies)
    forward_mid = join(nt(residual_mid, mid_f[0]), nt(residual_mid, mid_f[1])).astype(BF16)

    def sum_over_y(part, out, into, sem):
        out[...] = part[...].astype(BF16)
        return [
            post(out, into.at[d], sem.at[d], y_mates[d]) for d in range(NY - 1)
        ]

    def total(part, into, copies):
        for copy in copies:
            copy.wait_recv()
        summed = part[...]
        for d in range(NY - 1):
            summed = summed + into[d].astype(F32)
        return summed.astype(BF16)

    root_copies = [relay(3)]
    complete(couple_copies[0])
    complete(couple_copies[1])
    root_part[...] = -join(nn(forward_mid, couple_f[0]), nn(forward_mid, couple_f[1]))
    root_part[0:SLICE, block_rows] += rhs_root_t
    copies = sum_over_y(root_part, root_send, root_recv, root_sem)
    root_copies.append(relay(4))
    pass_far(3, root_copies[0])
    pass_far(4, root_copies[1])
    residual_root = total(root_part, root_recv, copies)
    complete(root_copies[0])
    complete(root_copies[1])
    forward_root = join(nt(residual_root, root_f[0]), nt(residual_root, root_f[1])).astype(BF16)
    root_part[...] = join(nn(forward_root, root_f[0]), nn(forward_root, root_f[1]))
    copies = sum_over_y(root_part, back_send, back_recv, back_sem)
    x_root[...] = total(root_part, back_recv, copies)

    from_root = join(nt(x_root[...], couple_f[0]), nt(x_root[...], couple_f[1]))
    update_mid = (forward_mid.astype(F32) - from_root).astype(BF16)
    mid_part[...] = join(nn(update_mid, mid_f[0]), nn(update_mid, mid_f[1]))
    xmid_send[...] = mid_part[...].astype(BF16)
    xmid_copy = post(xmid_send, xmid_recv, xmid_sem, partner)
    xmid_copy.wait_recv()
    x_mid[...] = (mid_part[...] + xmid_recv[...].astype(F32)).astype(BF16)
    picked_send[...] = nn(x_mid[...], places[...]).astype(BF16).reshape(2, SLICE, NZ * COUPLE)
    for d in range(NZ):
        zl = lax.rem(z + d, NZ)
        post_or_keep(
            picked_send.at[:, :, pl.ds(pl.multiple_of(zl * COUPLE, COUPLE), COUPLE)],
            picked.at[point, :, pl.ds(pl.multiple_of(group * SLICE, SLICE), SLICE), :],
            picked_sem,
            home,
            zl,
        )

    small_send[:, 0:BLOCK] = x_root[:, block_rows]
    small_send[:, BLOCK:] = x_mid[:, half_rows]
    small_copies = [
        post(small_send, small_recv.at[d], small_sem.at[d], x_mates[d]) for d in range(NX - 1)
    ]

    arrived(picked, picked_sem)
    for q in range(2):
        picked_q = picked[q].reshape(2 * PROBES, COUPLE)
        for n in range(2):
            columns = slice(n * 512, (n + 1) * 512)
            change = join(nn(picked_q, couple_v[q, 0, :, columns]), nn(picked_q, couple_v[q, 1, :, columns]))
            live = lax.broadcasted_iota(jnp.int32, change.shape, 1) + n * 512 < size
            update[q, :, columns] = jnp.where(
                live, forward[q, :, columns].astype(F32) - change, 0.0
            ).astype(BF16)

    first = 2 * quad

    core_base, chip_base = counter[0], counter[0] + CHUNKS
    counter[0] += CHUNKS + CHUNKS * (NX - 1)

    def core_copy(i):
        return pltpu.make_async_remote_copy(
            src_ref=core_send.at[i],
            dst_ref=core_recv.at[i],
            send_sem=send_sem.at[core_base + i],
            recv_sem=core_sem.at[i],
            device_id=sibling,
            device_id_type=MESH,
        )

    def chip_copy(i, d):
        return pltpu.make_async_remote_copy(
            src_ref=chip_send.at[i, d],
            dst_ref=chip_recv.at[i, d],
            send_sem=send_sem.at[chip_base + i * (NX - 1) + d],
            recv_sem=chip_sem.at[i, d],
            device_id=x_mates[d],
            device_id_type=MESH,
        )

    def leaf_step(i):
        columns = pl.ds(pl.multiple_of(i * CHUNK, CHUNK), CHUNK)
        for q in range(2):
            solved = join(
                nn(update[q], inv_v[q, 0, :, columns]), nn(update[q], inv_v[q, 1, :, columns])
            )
            live = lax.broadcasted_iota(jnp.int32, solved.shape, 1) + i * CHUNK < size
            parts[pl.ds(2 * q * PROBES, 2 * PROBES), :] = jnp.where(live, solved, 0.0)

        def moment(k):
            total_k = None
            for q in range(2):
                for a in range(2):
                    row = (2 * q + a) * PROBES
                    term = weights[first + q, 2 * k + a] * parts[row : row + PROBES, :]
                    total_k = term if total_k is None else total_k + term
            return total_k

        for xx in range(NX):
            core_send[i, xx] = moment(2 * xx + 1 - c).astype(BF16)
            own_sum[i, xx] = moment(2 * xx + c)
        core_copy(i).start()

    def chip_step(i):
        core_copy(i).wait_recv()
        chip_own[i] = own_sum[i, x] + core_recv[i, x].astype(F32)
        for d in range(NX - 1):
            xx = lax.rem(x + d + 1, NX)
            chip_send[i, d] = (own_sum[i, xx] + core_recv[i, xx].astype(F32)).astype(BF16)
            chip_copy(i, d).start()

    def tail_step(i, carry):
        leaf_step(i)

        @pl.when(i > 0)
        def _():
            chip_step(i - 1)

        return carry

    lax.fori_loop(0, CHUNKS, tail_step, 0)
    chip_step(CHUNKS - 1)

    for copy in small_copies:
        copy.wait_recv()
    hosted = lax.div(z, 2)
    pieces = [small_send[...].astype(F32)] + [small_recv[d].astype(F32) for d in range(NX - 1)]
    spread[...] = jnp.zeros_like(spread)
    for cc in range(NC):
        total_k = None
        for d in range(NX):
            point_d = 4 * lax.rem(x + NX - d, NX) + hosted
            real = weights[point_d, 2 * (2 * x + cc)] * pieces[d][0:SLICE]
            imag = weights[point_d, 2 * (2 * x + cc) + 1] * pieces[d][SLICE:]
            total_k = real + imag if total_k is None else total_k + (real + imag)
        spread[pl.ds(pl.multiple_of(group * SLICE, SLICE), SLICE), :] = total_k
        rows_send[cc] = spread[...].T.astype(BF16).reshape(2, BLOCK, PROBES)
    for i in range(NC * NZ):
        place = lax.rem(c * NZ + z + i, NC * NZ)
        cc, zz = lax.div(place, NZ), lax.rem(place, NZ)
        src = rows_send.at[cc, :, pl.ds(pl.multiple_of(zz * OWN, OWN), OWN), :]
        dst = rows_recv.at[i]
        if i == 0:
            pltpu.make_async_copy(src, dst, rows_sem).start()
        else:
            post(src, dst, rows_sem, device(x, cc, y, zz))
    arrived(rows_recv, rows_sem)
    gathered = rows_recv[0].astype(F32)
    for i in range(1, NC * NZ):
        gathered = gathered + rows_recv[i].astype(F32)
    out_root[0] = gathered[0]
    out_mid[0] = gathered[1]

    for i in range(CHUNKS):
        result = chip_own[i]
        for d in range(NX - 1):
            chip_copy(i, d).wait_recv()
            result = result + chip_recv[i, d].astype(F32)
        out_leaf[0, i * CHUNK : (i + 1) * CHUNK, :] = result.T

    for mine, copy in sends:
        if mine is None:
            copy.wait_send()
        else:

            @pl.when(jnp.logical_not(mine))
            def _():
                copy.wait_send()

    for i in range(CHUNKS):
        core_copy(i).wait_send()
        for d in range(NX - 1):
            chip_copy(i, d).wait_send()


def deliver(leaf, mid, root, out_leaf, out_mid, out_root):
    out_leaf[...] = leaf[...]
    out_mid[...] = mid[...]
    out_root[...] = root[...]


def weight_table():
    table = np.zeros((QPOINTS, 2 * MOMENTS), np.float32)
    for q in range(QPOINTS):
        for k in range(MOMENTS):
            angle = 2.0 * math.pi * (q + 0.5) / QPOINTS * (k + 1)
            table[q, 2 * k] = 4.0 / QPOINTS * math.cos(angle)
            table[q, 2 * k + 1] = -4.0 / QPOINTS * math.sin(angle)
    return jnp.asarray(table)


def body(*arrays):
    vmem = pl.BlockSpec(memory_space=pltpu.VMEM)
    hbm = pl.BlockSpec(memory_space=pltpu.HBM)
    in_specs = [hbm] * 11
    out_shape = [
        jax.ShapeDtypeStruct((1, LEAF, PROBES), F32),
        jax.ShapeDtypeStruct((1, OWN, PROBES), F32),
        jax.ShapeDtypeStruct((1, OWN, PROBES), F32),
    ]
    cols = 2 * SLICE
    dma = pltpu.SemaphoreType.DMA
    scratch = [
        pltpu.VMEM((LEAF, PROBES), BF16),
        pltpu.SMEM((1,), jnp.int32),
        pltpu.SMEM((QPOINTS, 2 * MOMENTS), F32),
        pltpu.VMEM((2, 2, LEAF, LEAF), BF16),
        pltpu.VMEM((2, 2, COUPLE, LEAF), BF16),
        pltpu.VMEM((LEAF, PROBES), BF16),
        pltpu.VMEM((2, LEAF, 2 * PROBES), BF16),
        pltpu.VMEM((2, 2 * PROBES, LEAF), BF16),
        pltpu.VMEM((2, 2 * PROBES, LEAF), BF16),
        pltpu.VMEM((2, BLOCK, SEP), BF16),
        pltpu.VMEM((2, BLOCK, ROOT), BF16),
        pltpu.VMEM((2, BLOCK, ROOT), BF16),
        pltpu.VMEM((SEP, NZ * COUPLE), BF16),
        pltpu.VMEM((1, COUPLE), jnp.int32),
        pltpu.VMEM((SHARED, PROBES), BF16),
        pltpu.VMEM((NZ, SHARED, PROBES), BF16),
        pltpu.VMEM((NZ, OWN, PROBES), BF16),
        pltpu.VMEM((2, 2, PROBES, COUPLE), BF16),
        pltpu.VMEM((2, SLICE, NZ * COUPLE), BF16),
        pltpu.VMEM((cols, SEP), F32),
        pltpu.VMEM((cols, SEP), BF16),
        pltpu.VMEM((cols, SEP), BF16),
        pltpu.VMEM((cols, ROOT), F32),
        pltpu.VMEM((cols, ROOT), BF16),
        pltpu.VMEM((NY - 1, cols, ROOT), BF16),
        pltpu.VMEM((cols, ROOT), BF16),
        pltpu.VMEM((NY - 1, cols, ROOT), BF16),
        pltpu.VMEM((cols, ROOT), BF16),
        pltpu.VMEM((cols, SEP), BF16),
        pltpu.VMEM((cols, SEP), BF16),
        pltpu.VMEM((cols, SEP), BF16),
        pltpu.VMEM((2, SLICE, NZ * COUPLE), BF16),
        pltpu.VMEM((2, 2, PROBES, COUPLE), BF16),
        pltpu.VMEM((4 * PROBES, CHUNK), F32),
        pltpu.VMEM((CHUNKS, NX, PROBES, CHUNK), F32),
        pltpu.VMEM((CHUNKS, NX, PROBES, CHUNK), BF16),
        pltpu.VMEM((CHUNKS, NX, PROBES, CHUNK), BF16),
        pltpu.VMEM((CHUNKS, PROBES, CHUNK), F32),
        pltpu.VMEM((CHUNKS, NX - 1, PROBES, CHUNK), BF16),
        pltpu.VMEM((CHUNKS, NX - 1, PROBES, CHUNK), BF16),
        pltpu.VMEM((cols, 2 * BLOCK), BF16),
        pltpu.VMEM((NX - 1, cols, 2 * BLOCK), BF16),
        pltpu.VMEM((PROBES, 2 * BLOCK), F32),
        pltpu.VMEM((NC, 2, BLOCK, PROBES), BF16),
        pltpu.VMEM((NC * NZ, 2, OWN, PROBES), BF16),
        dma((5,)),
        dma((4,)),
        dma,
        dma,
        dma,
        dma((5,)),
        dma((5,)),
        dma((5, 2)),
        dma,
        dma,
        dma((NY - 1,)),
        dma((NY - 1,)),
        dma,
        dma,
        dma((CHUNKS,)),
        dma((CHUNKS, NX - 1)),
        dma((NX - 1,)),
        dma,
        dma((128,)),
    ]
    results = pl.pallas_call(
        kernel,
        out_shape=out_shape,
        in_specs=in_specs,
        out_specs=[vmem, vmem, vmem],
        scratch_shapes=scratch,
        compiler_params=pltpu.CompilerParams(
            collective_id=0, has_side_effects=True, vmem_limit_bytes=56 * 2**20
        ),
    )(*arrays, weight_table())
    return tuple(
        pl.pallas_call(
            deliver,
            out_shape=out_shape,
            in_specs=[vmem] * 3,
            out_specs=[vmem] * 3,
        )(*results)
    )


def solution(mesh):
    in_specs = (
        P("leaf", None),
        P("leaf", None),
        P("leaf", None),
        P("quad", None, "leaf", None),
        P("quad", None, "leaf", None),
        P("leaf", None),
        P("leaf"),
        P("quad", None, "leaf", None),
        P("quad", None, "leaf", None),
        P("quad", None, "leaf", None),
    )
    out_specs = (P("quad", "leaf", None), P("quad", "leaf", None), P("quad", "leaf", None))
    return jax.shard_map(body, mesh=mesh, in_specs=in_specs, out_specs=out_specs, check_vma=False)
```

```python
import functools
import math

import jax
import jax.numpy as jnp
import numpy as np
from jax import lax
from jax.experimental import pallas as pl
from jax.experimental.pallas import tpu as pltpu
from jax.sharding import PartitionSpec as P

MESH = pl.DeviceIdType.MESH
BF16 = jnp.bfloat16
F32 = jnp.float32

MOMENTS = 8
QPOINTS = 16
PROBES = 128
LEAF = 1024
COUPLE = 128
SEP = 512
ROOT = 1024
NX, NY, NZ, NC = 4, 4, 8, 2
OWN = 32
BLOCK = OWN * NZ
SLICE = 32
SHARED = OWN + 16
CHUNK = 256
CHUNKS = LEAF // CHUNK


def nt(left, right):
    return lax.dot_general(left, right, (((1,), (1,)), ((), ())), preferred_element_type=F32)


def nn(left, right):
    return lax.dot_general(left, right, (((1,), (0,)), ((), ())), preferred_element_type=F32)


def join(with_real, with_imag):
    half = with_real.shape[0] // 2
    return jnp.concatenate(
        [with_real[:half] - with_imag[half:], with_real[half:] + with_imag[:half]], axis=0
    )


def kernel(
    rhs_leaf_h,
    rhs_mid,
    rhs_root,
    leaf_inv,
    leaf_couple,
    row_list,
    leaf_size_h,
    mid_inv,
    mid_root,
    root_inv,
    weights_h,
    out_leaf,
    out_mid,
    out_root,
    rhs_leaf,
    leaf_size,
    weights,
    inv_v,
    couple_v,
    source,
    solved_rows,
    forward,
    update,
    mid_f,
    couple_f,
    root_f,
    places,
    list_v,
    shared,
    shared_y,
    other_y,
    terms,
    terms_in,
    mid_part,
    mid_send,
    mid_recv,
    root_part,
    root_send,
    root_recv,
    back_send,
    back_recv,
    x_root,
    xmid_send,
    xmid_recv,
    x_mid,
    picked_send,
    picked,
    parts,
    own_sum,
    core_send,
    core_recv,
    chip_own,
    chip_send,
    chip_recv,
    small_send,
    small_recv,
    spread,
    rows_send,
    rows_recv,
    load_sem,
    inv_sem,
    couple_sem,
    shared_sem,
    other_sem,
    block_sem,
    relay_sem,
    pass_sem,
    terms_sem,
    mid_sem,
    root_sem,
    back_sem,
    xmid_sem,
    picked_sem,
    core_sem,
    chip_sem,
    small_sem,
    rows_sem,
    send_sem,
):
    quad, leaf = lax.axis_index("quad"), lax.axis_index("leaf")
    x, c = lax.div(quad, 2), lax.rem(quad, 2)
    y, z = lax.div(leaf, NZ), lax.rem(leaf, NZ)
    home = lax.div(z, 4)
    point = lax.rem(lax.div(z, 2), 2)
    group = 2 * lax.rem(z, 2) + c
    half = lax.rem(y, 2)
    sends = []
    counter = [0]

    def device(xx, cc, yy, zz):
        return (2 * xx + cc, NZ * yy + zz)

    def send(src, dst, recv, target):
        copy = pltpu.make_async_remote_copy(
            src_ref=src,
            dst_ref=dst,
            send_sem=send_sem.at[counter[0]],
            recv_sem=recv,
            device_id=target,
            device_id_type=MESH,
        )
        counter[0] += 1
        return copy

    def post(src, dst, recv, target):
        copy = send(src, dst, recv, target)
        copy.start()
        sends.append((None, copy))
        return copy

    def post_or_keep(src, dst, recv, cc, zz):
        mine = jnp.logical_and(cc == c, zz == z)
        copy = send(src, dst, recv, device(x, cc, y, zz))

        @pl.when(mine)
        def _():
            pltpu.make_async_copy(src, dst, recv).start()

        @pl.when(jnp.logical_not(mine))
        def _():
            copy.start()

        sends.append((mine, copy))

    def arrived(buffer, sem):
        pltpu.make_async_copy(buffer, buffer, sem).wait()

    def spread_blocks(k):
        matrix, whole, columns = pieces[k]
        for q in range(2):
            slot = lax.rem(z - 2 * (2 * c + q) + 3 + NZ, NZ)
            near = 2 * (2 * c + q) + lax.div(slot, 4)
            for cc in range(NC):
                post_or_keep(
                    matrix.at[q, cc, :, columns],
                    whole.at[cc, pl.ds(pl.multiple_of(slot * OWN, OWN), OWN), columns],
                    block_sem.at[k],
                    cc,
                    near,
                )

    first_half, second_half = pl.ds(0, ROOT // 2), pl.ds(ROOT // 2, ROOT // 2)
    pieces = (
        (mid_inv, mid_f, pl.ds(0, SEP)),
        (mid_root, couple_f, first_half),
        (mid_root, couple_f, second_half),
        (root_inv, root_f, first_half),
        (root_inv, root_f, second_half),
    )
    side = lax.rem(z, 2)
    pair = device(x, c, y, z + 1 - 2 * side)
    sibling = device(x, 1 - c, y, z)
    near_rows = pl.ds(pl.multiple_of(side * (BLOCK // 2), BLOCK // 2), BLOCK // 2)
    far_rows = pl.ds(pl.multiple_of((1 - side) * (BLOCK // 2), BLOCK // 2), BLOCK // 2)

    def relay(k):
        rows = pieces[k][1].at[c, near_rows, pieces[k][2]]
        arrived(rows, block_sem.at[k])
        return [
            post(rows, rows, relay_sem.at[k], pair),
            post(rows, rows, pass_sem.at[k, 0], sibling),
        ]

    def pass_far(k, copies):
        copies[0].wait_recv()
        rows = pieces[k][1].at[c, far_rows, pieces[k][2]]
        copies.append(post(rows, rows, pass_sem.at[k, 1], sibling))

    def complete(copies):
        copies[1].wait_recv()
        copies[2].wait_recv()

    loads = [
        pltpu.make_async_copy(leaf_size_h, leaf_size, load_sem.at[0]),
        pltpu.make_async_copy(rhs_leaf_h, rhs_leaf, load_sem.at[1]),
        pltpu.make_async_copy(weights_h, weights, load_sem.at[2]),
        pltpu.make_async_copy(row_list, list_v, load_sem.at[3]),
    ]
    for load in loads:
        load.start()
    mid_load = pltpu.make_async_copy(rhs_mid, shared.at[pl.ds(0, OWN)], load_sem.at[4])
    root_load = pltpu.make_async_copy(rhs_root, shared.at[pl.ds(0, OWN)], load_sem.at[4])

    @pl.when(c == 0)
    def _():
        mid_load.start()

    @pl.when(c == 1)
    def _():
        root_load.start()

    for i in range(4):
        block = (i // 2, i % 2)
        pltpu.make_async_copy(leaf_inv.at[block], inv_v.at[block], inv_sem.at[i]).start()
    couple_load = pltpu.make_async_copy(leaf_couple, couple_v, couple_sem)
    couple_load.start()

    barrier = pltpu.get_barrier_semaphore()
    mates = []
    for i in range(1, NC * NZ):
        place = lax.rem(c * NZ + z + i, NC * NZ)
        mates.append(device(x, lax.div(place, NZ), y, lax.rem(place, NZ)))
    y_mates = [device(x, c, lax.rem(y + d, NY), z) for d in range(1, NY)]
    x_mates = [device(lax.rem(x + d, NX), c, y, z) for d in range(1, NX)]
    for mate in mates + y_mates + x_mates:
        pl.semaphore_signal(barrier, inc=1, device_id=mate, device_id_type=MESH)

    for load in loads:
        load.wait()
    mid_load.wait()
    size = leaf_size[0]
    listed = jnp.broadcast_to(list_v[...], (16, COUPLE))
    high = lax.div(listed, 16)
    low = listed - 16 * high
    first_row = lax.broadcasted_iota(jnp.int32, (16, COUPLE), 0) == 0
    shared[OWN:SHARED, :] = jnp.where(first_row, high, low).astype(F32).astype(BF16)
    row_live = lax.broadcasted_iota(jnp.int32, (LEAF, PROBES), 0) < size
    source[...] = jnp.where(row_live, rhs_leaf[...].astype(F32), 0.0).astype(BF16)

    def forward_step(i, carry):
        q, a = lax.div(i, 2), lax.rem(i, 2)
        arrived(inv_v.at[q, a], inv_sem.at[i])
        product = nn(inv_v[q, a], source[...])
        live = lax.broadcasted_iota(jnp.int32, product.shape, 0) < size
        solved_rows[q, :, pl.ds(pl.multiple_of(a * PROBES, PROBES), PROBES)] = jnp.where(
            live, product, 0.0
        ).astype(BF16)
        return carry

    def couple_step(q):
        with_real = nn(couple_v[q, 0], solved_rows[q])
        with_imag = nn(couple_v[q, 1], solved_rows[q])
        terms[q, 0] = (with_real[:, :PROBES] - with_imag[:, PROBES:]).T.astype(BF16)
        terms[q, 1] = (with_real[:, PROBES:] + with_imag[:, :PROBES]).T.astype(BF16)

    def terms_out(q):
        for t in (2 * q, 2 * q + 1):
            for cc in range(NC):
                pg = 2 * (t % 2) + cc
                post_or_keep(
                    terms.at[q, :, pl.ds(pg * SLICE, SLICE), :],
                    terms_in.at[:, :, pl.ds(pl.multiple_of(z * COUPLE, COUPLE), COUPLE)],
                    terms_sem,
                    cc,
                    4 * c + t,
                )

    lax.fori_loop(0, 4, forward_step, 0)
    couple_load.wait()
    couple_step(0)
    couple_step(1)
    pl.semaphore_wait(barrier, len(mates) + len(y_mates) + len(x_mates))

    spread_blocks(1)
    terms_out(0)
    terms_out(1)
    spread_blocks(2)
    spread_blocks(0)
    pltpu.make_async_copy(shared, shared_y.at[z], shared_sem).start()
    for d in range(1, NZ):
        post(shared, shared_y.at[z], shared_sem, device(x, c, y, lax.rem(z + d, NZ)))

    couple_copies = [relay(1), relay(2)]
    spread_blocks(3)
    spread_blocks(4)
    mid_copies = relay(0)
    arrived(shared_y, shared_sem)
    other_copy = post(shared_y.at[:, pl.ds(0, OWN)], other_y, other_sem, sibling)
    for l in range(NZ):
        sep_row = lax.broadcasted_iota(jnp.int32, (SEP, COUPLE), 0)
        codes = shared_y[l, OWN:SHARED, :].astype(F32)
        listed = (16.0 * codes[0:1] + codes[1:2]).astype(jnp.int32)
        places[:, l * COUPLE : (l + 1) * COUPLE] = (
            jnp.where(sep_row == listed, 1.0, 0.0).astype(BF16)
        )
    chosen = jnp.where(
        lax.broadcasted_iota(jnp.int32, (SLICE, PROBES), 1)
        == lax.broadcasted_iota(jnp.int32, (SLICE, PROBES), 0) + group * SLICE,
        1.0,
        0.0,
    ).astype(BF16)
    other_copy.wait_recv()
    mine_t = nt(chosen, shared_y[:, 0:OWN, :].reshape(BLOCK, PROBES))
    other_t = nt(chosen, other_y[...].reshape(BLOCK, PROBES))
    rhs_mid_t = jnp.where(c == 0, mine_t, other_t)
    rhs_root_t = jnp.where(c == 0, other_t, mine_t)

    for q in range(2):
        forward[q] = solved_rows[q].T

    half_rows = pl.ds(pl.multiple_of(half * BLOCK, BLOCK), BLOCK)
    block_rows = pl.ds(pl.multiple_of(y * BLOCK, BLOCK), BLOCK)
    partner = device(x, c, y + 1 - 2 * half, z)
    arrived(terms_in, terms_sem)
    mid_part[...] = -nt(terms_in[...].reshape(2 * SLICE, NZ * COUPLE), places[...])
    mid_part[0:SLICE, half_rows] += rhs_mid_t
    mid_send[...] = mid_part[...].astype(BF16)
    mid_copy = post(mid_send, mid_recv, mid_sem, partner)
    pass_far(1, couple_copies[0])
    pass_far(2, couple_copies[1])
    pass_far(0, mid_copies)
    mid_copy.wait_recv()
    residual_mid = (mid_part[...] + mid_recv[...].astype(F32)).astype(BF16)
    complete(mid_copies)
    forward_mid = join(nt(residual_mid, mid_f[0]), nt(residual_mid, mid_f[1])).astype(BF16)

    def sum_over_y(part, out, into, sem):
        out[...] = part[...].astype(BF16)
        return [
            post(out, into.at[d], sem.at[d], y_mates[d]) for d in range(NY - 1)
        ]

    def total(part, into, copies):
        for copy in copies:
            copy.wait_recv()
        summed = part[...]
        for d in range(NY - 1):
            summed = summed + into[d].astype(F32)
        return summed.astype(BF16)

    root_copies = [relay(3)]
    complete(couple_copies[0])
    complete(couple_copies[1])
    root_part[...] = -join(nn(forward_mid, couple_f[0]), nn(forward_mid, couple_f[1]))
    root_part[0:SLICE, block_rows] += rhs_root_t
    copies = sum_over_y(root_part, root_send, root_recv, root_sem)
    root_copies.append(relay(4))
    pass_far(3, root_copies[0])
    pass_far(4, root_copies[1])
    residual_root = total(root_part, root_recv, copies)
    complete(root_copies[0])
    complete(root_copies[1])
    forward_root = join(nt(residual_root, root_f[0]), nt(residual_root, root_f[1])).astype(BF16)
    root_part[...] = join(nn(forward_root, root_f[0]), nn(forward_root, root_f[1]))
    copies = sum_over_y(root_part, back_send, back_recv, back_sem)
    x_root[...] = total(root_part, back_recv, copies)

    from_root = join(nt(x_root[...], couple_f[0]), nt(x_root[...], couple_f[1]))
    update_mid = (forward_mid.astype(F32) - from_root).astype(BF16)
    mid_part[...] = join(nn(update_mid, mid_f[0]), nn(update_mid, mid_f[1]))
    xmid_send[...] = mid_part[...].astype(BF16)
    xmid_copy = post(xmid_send, xmid_recv, xmid_sem, partner)
    xmid_copy.wait_recv()
    x_mid[...] = (mid_part[...] + xmid_recv[...].astype(F32)).astype(BF16)
    picked_send[...] = nn(x_mid[...], places[...]).astype(BF16).reshape(2, SLICE, NZ * COUPLE)
    for d in range(NZ):
        zl = lax.rem(z + d, NZ)
        post_or_keep(
            picked_send.at[:, :, pl.ds(pl.multiple_of(zl * COUPLE, COUPLE), COUPLE)],
            picked.at[point, :, pl.ds(pl.multiple_of(group * SLICE, SLICE), SLICE), :],
            picked_sem,
            home,
            zl,
        )

    small_send[:, 0:BLOCK] = x_root[:, block_rows]
    small_send[:, BLOCK:] = x_mid[:, half_rows]
    small_copies = [
        post(small_send, small_recv.at[d], small_sem.at[d], x_mates[d]) for d in range(NX - 1)
    ]

    arrived(picked, picked_sem)
    for q in range(2):
        picked_q = picked[q].reshape(2 * PROBES, COUPLE)
        for n in range(2):
            columns = slice(n * 512, (n + 1) * 512)
            change = join(nn(picked_q, couple_v[q, 0, :, columns]), nn(picked_q, couple_v[q, 1, :, columns]))
            live = lax.broadcasted_iota(jnp.int32, change.shape, 1) + n * 512 < size
            update[q, :, columns] = jnp.where(
                live, forward[q, :, columns].astype(F32) - change, 0.0
            ).astype(BF16)

    first = 2 * quad

    core_base, chip_base = counter[0], counter[0] + CHUNKS
    counter[0] += CHUNKS + CHUNKS * (NX - 1)

    def core_copy(i):
        return pltpu.make_async_remote_copy(
            src_ref=core_send.at[i],
            dst_ref=core_recv.at[i],
            send_sem=send_sem.at[core_base + i],
            recv_sem=core_sem.at[i],
            device_id=sibling,
            device_id_type=MESH,
        )

    def chip_copy(i, d):
        return pltpu.make_async_remote_copy(
            src_ref=chip_send.at[i, d],
            dst_ref=chip_recv.at[i, d],
            send_sem=send_sem.at[chip_base + i * (NX - 1) + d],
            recv_sem=chip_sem.at[i, d],
            device_id=x_mates[d],
            device_id_type=MESH,
        )

    def leaf_step(i):
        columns = pl.ds(pl.multiple_of(i * CHUNK, CHUNK), CHUNK)
        for q in range(2):
            solved = join(
                nn(update[q], inv_v[q, 0, :, columns]), nn(update[q], inv_v[q, 1, :, columns])
            )
            live = lax.broadcasted_iota(jnp.int32, solved.shape, 1) + i * CHUNK < size
            parts[pl.ds(2 * q * PROBES, 2 * PROBES), :] = jnp.where(live, solved, 0.0)

        def moment(k):
            total_k = None
            for q in range(2):
                for a in range(2):
                    row = (2 * q + a) * PROBES
                    term = weights[first + q, 2 * k + a] * parts[row : row + PROBES, :]
                    total_k = term if total_k is None else total_k + term
            return total_k

        for xx in range(NX):
            core_send[i, xx] = moment(2 * xx + 1 - c).astype(BF16)
            own_sum[i, xx] = moment(2 * xx + c)
        core_copy(i).start()

    def chip_step(i):
        core_copy(i).wait_recv()
        chip_own[i] = own_sum[i, x] + core_recv[i, x].astype(F32)
        for d in (1, 0, 2):
            xx = lax.rem(x + d + 1, NX)
            chip_send[i, d] = (own_sum[i, xx] + core_recv[i, xx].astype(F32)).astype(BF16)
            chip_copy(i, d).start()

    def tail_step(i, carry):
        leaf_step(i)

        @pl.when(i > 0)
        def _():
            chip_step(i - 1)

        return carry

    lax.fori_loop(0, CHUNKS, tail_step, 0)
    chip_step(CHUNKS - 1)

    for copy in small_copies:
        copy.wait_recv()
    hosted = lax.div(z, 2)
    pieces = [small_send[...].astype(F32)] + [small_recv[d].astype(F32) for d in range(NX - 1)]
    spread[...] = jnp.zeros_like(spread)
    for cc in range(NC):
        total_k = None
        for d in range(NX):
            point_d = 4 * lax.rem(x + NX - d, NX) + hosted
            real = weights[point_d, 2 * (2 * x + cc)] * pieces[d][0:SLICE]
            imag = weights[point_d, 2 * (2 * x + cc) + 1] * pieces[d][SLICE:]
            total_k = real + imag if total_k is None else total_k + (real + imag)
        spread[pl.ds(pl.multiple_of(group * SLICE, SLICE), SLICE), :] = total_k
        rows_send[cc] = spread[...].T.astype(BF16).reshape(2, BLOCK, PROBES)
    for i in range(NC * NZ):
        place = lax.rem(c * NZ + z + i, NC * NZ)
        cc, zz = lax.div(place, NZ), lax.rem(place, NZ)
        src = rows_send.at[cc, :, pl.ds(pl.multiple_of(zz * OWN, OWN), OWN), :]
        dst = rows_recv.at[i]
        if i == 0:
            pltpu.make_async_copy(src, dst, rows_sem).start()
        else:
            post(src, dst, rows_sem, device(x, cc, y, zz))
    arrived(rows_recv, rows_sem)
    gathered = rows_recv[0].astype(F32)
    for i in range(1, NC * NZ):
        gathered = gathered + rows_recv[i].astype(F32)
    out_root[0] = gathered[0]
    out_mid[0] = gathered[1]

    for i in range(CHUNKS):
        result = chip_own[i]
        for d in range(NX - 1):
            chip_copy(i, d).wait_recv()
            result = result + chip_recv[i, d].astype(F32)
        out_leaf[0, i * CHUNK : (i + 1) * CHUNK, :] = result.T

    for mine, copy in sends:
        if mine is None:
            copy.wait_send()
        else:

            @pl.when(jnp.logical_not(mine))
            def _():
                copy.wait_send()

    for i in range(CHUNKS):
        core_copy(i).wait_send()
        for d in range(NX - 1):
            chip_copy(i, d).wait_send()


def deliver(leaf, mid, root, out_leaf, out_mid, out_root):
    out_leaf[...] = leaf[...]
    out_mid[...] = mid[...]
    out_root[...] = root[...]


def weight_table():
    table = np.zeros((QPOINTS, 2 * MOMENTS), np.float32)
    for q in range(QPOINTS):
        for k in range(MOMENTS):
            angle = 2.0 * math.pi * (q + 0.5) / QPOINTS * (k + 1)
            table[q, 2 * k] = 4.0 / QPOINTS * math.cos(angle)
            table[q, 2 * k + 1] = -4.0 / QPOINTS * math.sin(angle)
    return jnp.asarray(table)


def body(*arrays):
    vmem = pl.BlockSpec(memory_space=pltpu.VMEM)
    hbm = pl.BlockSpec(memory_space=pltpu.HBM)
    in_specs = [hbm] * 11
    out_shape = [
        jax.ShapeDtypeStruct((1, LEAF, PROBES), F32),
        jax.ShapeDtypeStruct((1, OWN, PROBES), F32),
        jax.ShapeDtypeStruct((1, OWN, PROBES), F32),
    ]
    cols = 2 * SLICE
    dma = pltpu.SemaphoreType.DMA
    scratch = [
        pltpu.VMEM((LEAF, PROBES), BF16),
        pltpu.SMEM((1,), jnp.int32),
        pltpu.SMEM((QPOINTS, 2 * MOMENTS), F32),
        pltpu.VMEM((2, 2, LEAF, LEAF), BF16),
        pltpu.VMEM((2, 2, COUPLE, LEAF), BF16),
        pltpu.VMEM((LEAF, PROBES), BF16),
        pltpu.VMEM((2, LEAF, 2 * PROBES), BF16),
        pltpu.VMEM((2, 2 * PROBES, LEAF), BF16),
        pltpu.VMEM((2, 2 * PROBES, LEAF), BF16),
        pltpu.VMEM((2, BLOCK, SEP), BF16),
        pltpu.VMEM((2, BLOCK, ROOT), BF16),
        pltpu.VMEM((2, BLOCK, ROOT), BF16),
        pltpu.VMEM((SEP, NZ * COUPLE), BF16),
        pltpu.VMEM((1, COUPLE), jnp.int32),
        pltpu.VMEM((SHARED, PROBES), BF16),
        pltpu.VMEM((NZ, SHARED, PROBES), BF16),
        pltpu.VMEM((NZ, OWN, PROBES), BF16),
        pltpu.VMEM((2, 2, PROBES, COUPLE), BF16),
        pltpu.VMEM((2, SLICE, NZ * COUPLE), BF16),
        pltpu.VMEM((cols, SEP), F32),
        pltpu.VMEM((cols, SEP), BF16),
        pltpu.VMEM((cols, SEP), BF16),
        pltpu.VMEM((cols, ROOT), F32),
        pltpu.VMEM((cols, ROOT), BF16),
        pltpu.VMEM((NY - 1, cols, ROOT), BF16),
        pltpu.VMEM((cols, ROOT), BF16),
        pltpu.VMEM((NY - 1, cols, ROOT), BF16),
        pltpu.VMEM((cols, ROOT), BF16),
        pltpu.VMEM((cols, SEP), BF16),
        pltpu.VMEM((cols, SEP), BF16),
        pltpu.VMEM((cols, SEP), BF16),
        pltpu.VMEM((2, SLICE, NZ * COUPLE), BF16),
        pltpu.VMEM((2, 2, PROBES, COUPLE), BF16),
        pltpu.VMEM((4 * PROBES, CHUNK), F32),
        pltpu.VMEM((CHUNKS, NX, PROBES, CHUNK), F32),
        pltpu.VMEM((CHUNKS, NX, PROBES, CHUNK), BF16),
        pltpu.VMEM((CHUNKS, NX, PROBES, CHUNK), BF16),
        pltpu.VMEM((CHUNKS, PROBES, CHUNK), F32),
        pltpu.VMEM((CHUNKS, NX - 1, PROBES, CHUNK), BF16),
        pltpu.VMEM((CHUNKS, NX - 1, PROBES, CHUNK), BF16),
        pltpu.VMEM((cols, 2 * BLOCK), BF16),
        pltpu.VMEM((NX - 1, cols, 2 * BLOCK), BF16),
        pltpu.VMEM((PROBES, 2 * BLOCK), F32),
        pltpu.VMEM((NC, 2, BLOCK, PROBES), BF16),
        pltpu.VMEM((NC * NZ, 2, OWN, PROBES), BF16),
        dma((5,)),
        dma((4,)),
        dma,
        dma,
        dma,
        dma((5,)),
        dma((5,)),
        dma((5, 2)),
        dma,
        dma,
        dma((NY - 1,)),
        dma((NY - 1,)),
        dma,
        dma,
        dma((CHUNKS,)),
        dma((CHUNKS, NX - 1)),
        dma((NX - 1,)),
        dma,
        dma((128,)),
    ]
    results = pl.pallas_call(
        kernel,
        out_shape=out_shape,
        in_specs=in_specs,
        out_specs=[vmem, vmem, vmem],
        scratch_shapes=scratch,
        compiler_params=pltpu.CompilerParams(
            collective_id=0, has_side_effects=True, vmem_limit_bytes=56 * 2**20
        ),
    )(*arrays, weight_table())
    return tuple(
        pl.pallas_call(
            deliver,
            out_shape=out_shape,
            in_specs=[vmem] * 3,
            out_specs=[vmem] * 3,
        )(*results)
    )


def solution(mesh):
    in_specs = (
        P("leaf", None),
        P("leaf", None),
        P("leaf", None),
        P("quad", None, "leaf", None),
        P("quad", None, "leaf", None),
        P("leaf", None),
        P("leaf"),
        P("quad", None, "leaf", None),
        P("quad", None, "leaf", None),
        P("quad", None, "leaf", None),
    )
    out_specs = (P("quad", "leaf", None), P("quad", "leaf", None), P("quad", "leaf", None))
    return jax.shard_map(body, mesh=mesh, in_specs=in_specs, out_specs=out_specs, check_vma=False)
```
